128 devices in a mesh: scen: 2 (over x_hi), hour: 16 (over z, y), reg: 4 (over x_lo, core).
Axes of the slice: x: 4 (x_hi: 2, x_lo: 2; x = x_hi * 2 + x_lo), y: 4, z: 4, core: 2. Of those that a mesh axis runs over, the one named last changes fastest.
Arguments:
- cost_rate: float32 [8, 2688, 2048], P('scen', 'hour', 'reg'), may hold values from 0.05 to 1
- invest_cost: float32 [3, 2048], P(None, 'reg'), may hold values from 0.1 to 1
- tile: bfloat16 [16, 256, 2048], P('hour', None, 'reg'), may hold values from -0.1875 to 0.1875
- tile_mask: int32 [16, 256, 2048], P('hour', None, 'reg'), may hold values 0 or 1
- demand: float32 [8, 2688, 256], P('scen', 'hour'), may hold values from -6 to 6
- dispatch: float32 [8, 2688, 2048], P('scen', 'hour', 'reg'), may hold values from 0 to 1
- dual: float32 [8, 2688, 256], P('scen', 'hour'), may hold values from 0 to 1
- cap_dual: float32 [8, 2688, 2048], P('scen', 'hour', 'reg'), may hold values from 0 to 1
- capacity: float32 [8, 3, 2048], P('scen', None, 'reg'), may hold values from 0 to 2
- multiplier: float32 [8, 3, 2048], P('scen', None, 'reg'), may hold values from -3 to 3
- consensus: float32 [8, 3, 2048], P('scen', None, 'reg'), may hold values from 0 to 2
- scen_weight: float32 [8], P('scen'), may hold values from 0.1 to 1
- node_of: int32 [3, 8], P(None, 'scen'), may hold values from 0 to 3, as said below
Outputs:
- dispatch_out: float32 [8, 2688, 2048], P('scen', 'hour', 'reg')
- dual_out: float32 [8, 2688, 256], P('scen', 'hour', 'reg')
- capacity_out: float32 [8, 3, 2048], P('scen', None, 'reg')
- multiplier_out: float32 [8, 3, 2048], P('scen', None, 'reg')
The draws below stay inside these ranges and needn't reach their ends.
Inputs may be any that keep to these rules, and one draw needn't show every extreme that they name: `node_of`: at each section the nodes are runs of consecutive scenarios, numbered in order from 0; each node of a section lies within one node of the section before; section 0 is one node, the last section has 4 nodes, and node counts grow from section to section.
All inputs are finite; a program needn't handle non-finite values. No bound on the sum of `tile_mask` on one device may be relied on, other than what follows from the above.
Results may differ from the reference program's by a relative error of at most 0.0015.
Values may be sent and summed in bfloat16 or wider, within the bound.
A program may use at most 64 MiB of HBM per device.

```python
import math
import jax
import jax.numpy as jnp
from jax import lax

COLS = 2048
CONS = 256
SECTIONS = 3
ITERS = 8
SCEN = 8
BLOCKS = 16
HOURS = 2688
NODES = 4


def draw_node_of(key, part):
    shuffled = jax.random.permutation(key, SCEN - 1) + 1
    section_rows = []
    for section in range(SECTIONS):
        node_count = 1 + (NODES - 1) * section // (SECTIONS - 1)
        boundary = jnp.zeros((SCEN,), jnp.int32).at[shuffled[:node_count - 1]].add(1)
        section_rows.append(jnp.cumsum(boundary))
    return jnp.stack(section_rows).astype(jnp.int32)


def with_ends(drawn, key, smallest, top_value):
    longest = drawn.shape.index(max(drawn.shape))
    spots = []
    for shift in (0, 1):
        where = [jax.random.randint(jax.random.fold_in(key, axis), (), 0, length) for axis, length in enumerate(drawn.shape)]
        where[longest] = (where[longest] + shift) % drawn.shape[longest]
        spots.append(tuple(where))
    return drawn.at[spots[0]].set(smallest).at[spots[1]].set(top_value)


def levels(stream_key, extent, pieces, least, high):
    factor_of = 1.0
    for axis_at, parts in pieces:
        steps = jax.random.uniform(jax.random.fold_in(jax.random.fold_in(stream_key, 6), axis_at), (parts,), jnp.float32, least / len(pieces), high / len(pieces))
        factor_of = factor_of * jnp.repeat(jnp.exp(steps), extent[axis_at] // parts).reshape((-1,) + (1,) * (len(extent) - 1 - axis_at))
    return factor_of


def bell_draw(own_key, shape, deviation, limit, split=(), kind=jnp.bfloat16):
    level = levels(own_key, shape, split, -0.22, 0.18) if split else 1.0
    entries = jax.random.normal(own_key, shape, jnp.float32) * deviation * level
    return jnp.minimum(jnp.maximum(entries, -limit), limit).astype(kind)


def setup_inputs(seed: int = 0) -> dict:
    streams_of = jax.random.split(jax.random.key(seed), 14)
    return {
        "cost_rate": jnp.clip(jnp.exp(math.log(1.0) - 2.9957323 * jax.random.uniform(streams_of[0], (SCEN, HOURS, COLS), jnp.float32) ** levels(streams_of[0], (SCEN, HOURS, COLS), ((0, 2), (1, 16), (2, 4)), -0.2, 0.2)), 0.05, 1.0),
        "invest_cost": jnp.clip(jnp.exp(math.log(1.0) - 2.3025851 * jax.random.uniform(streams_of[1], (SECTIONS, COLS), jnp.float32) ** levels(streams_of[1], (SECTIONS, COLS), ((1, 4),), -0.2, 0.2)), 0.1, 1.0),
        "tile": bell_draw(streams_of[2], (BLOCKS, CONS, COLS), (COLS // 2) ** -0.5, 0.1875, ((0, 16), (2, 4))),
        "tile_mask": with_ends((jax.random.randint(streams_of[3], (BLOCKS, CONS, COLS), 0, 2) < 1).astype(jnp.int32), jax.random.fold_in(streams_of[3], 1), 0, 1),
        "demand": bell_draw(streams_of[4], (SCEN, HOURS, CONS), 1.0, 6.0, ((0, 2), (1, 16)), jnp.float32),
        "dispatch": jnp.clip(1.0 * jax.random.uniform(streams_of[5], (SCEN, HOURS, COLS), jnp.float32) ** levels(streams_of[5], (SCEN, HOURS, COLS), ((0, 2), (1, 16), (2, 4)), -0.2, 0.2), 0.0, 1.0),
        "dual": jnp.clip(1.0 * jax.random.uniform(streams_of[6], (SCEN, HOURS, CONS), jnp.float32) ** levels(streams_of[6], (SCEN, HOURS, CONS), ((0, 2), (1, 16)), -0.2, 0.2), 0.0, 1.0),
        "cap_dual": jnp.clip(1.0 * jax.random.uniform(streams_of[7], (SCEN, HOURS, COLS), jnp.float32) ** levels(streams_of[7], (SCEN, HOURS, COLS), ((0, 2), (1, 16), (2, 4)), -0.2, 0.2), 0.0, 1.0),
        "capacity": jnp.clip(2.0 * jax.random.uniform(streams_of[8], (SCEN, SECTIONS, COLS), jnp.float32) ** levels(streams_of[8], (SCEN, SECTIONS, COLS), ((0, 2), (2, 4)), -0.2, 0.2), 0.0, 2.0),
        "multiplier": bell_draw(streams_of[9], (SCEN, SECTIONS, COLS), 0.5, 3.0, ((0, 2), (2, 4)), jnp.float32),
        "consensus": jnp.clip(2.0 * jax.random.uniform(streams_of[10], (SCEN, SECTIONS, COLS), jnp.float32) ** levels(streams_of[10], (SCEN, SECTIONS, COLS), ((0, 2), (2, 4)), -0.2, 0.2), 0.0, 2.0),
        "scen_weight": jnp.clip(jnp.exp(math.log(1.0) - 2.3025851 * jax.random.uniform(streams_of[11], (SCEN,), jnp.float32) ** levels(streams_of[11], (SCEN,), ((0, 2),), -0.2, 0.2)), 0.1, 1.0),
        "node_of": draw_node_of(jax.random.fold_in(streams_of[13], 71), 0),
    }


RAMP_WEIGHT = 0.5
PENALTY = 1.0
STEP_PRIMAL = 0.3
STEP_INVEST = 0.5
STEP_DUAL = 0.3
STEP_CAP = 0.05


def reference(cost_rate, invest_cost, tile, tile_mask, demand, dispatch, dual, cap_dual, capacity, multiplier, consensus, scen_weight, node_of):
    matrix = tile * tile_mask.astype(jnp.bfloat16)
    matrix_wide = matrix.astype(jnp.float32)
    nscen = dispatch.shape[0]
    nhours = dispatch.shape[1]
    nblocks = tile.shape[0]
    nblock_hours = nhours // nblocks
    primal = dispatch
    dual_var = dual
    cap_var = cap_dual
    invest = capacity
    for step_index in range(ITERS):
        dual_low = lax.optimization_barrier(dual_var.astype(jnp.bfloat16)).astype(jnp.float32)
        dual_four = dual_low.reshape(nscen, nblocks, nblock_hours, -1)
        pulled = jnp.einsum("sbhr,brc->sbhc", dual_four, matrix_wide).reshape(primal.shape)
        padded = jnp.pad(primal, ((0, 0), (1, 1), (0, 0)))
        rough = 2.0 * primal - padded[:, :-2] - padded[:, 2:]
        grad_x = cost_rate + RAMP_WEIGHT * rough - pulled + cap_var
        zmean = jnp.sum(cap_var, axis=1) / nhours
        grad_u = invest_cost[None] + multiplier + PENALTY * (invest - consensus) - zmean[:, None, :]
        primal_new = jnp.maximum(primal - STEP_PRIMAL * grad_x, 0.0)
        invest_new = jnp.maximum(invest - STEP_INVEST * grad_u, 0.0)
        primal_ext = 2.0 * primal_new - primal
        invest_ext = 2.0 * invest_new - invest
        ext_low = lax.optimization_barrier(primal_ext.astype(jnp.bfloat16)).astype(jnp.float32)
        ext_four = ext_low.reshape(nscen, nblocks, nblock_hours, -1)
        image = jnp.einsum("sbhc,brc->sbhr", ext_four, matrix_wide).reshape(dual_var.shape)
        dual_var = jnp.maximum(dual_var + STEP_DUAL * (demand - image), 0.0)
        cap_var = jnp.maximum(cap_var + STEP_CAP * (primal_ext - jnp.sum(invest_ext, axis=1)[:, None, :]), 0.0)
        primal = primal_new
        invest = invest_new
    node_ids = jnp.arange(NODES, dtype=jnp.int32)
    one_hot = (node_of[:, :, None] == node_ids[None, None, :]).astype(jnp.float32)
    weighted = scen_weight[:, None, None] * invest
    node_sum = jnp.einsum("gsn,sgc->gnc", one_hot, weighted, precision=lax.Precision.HIGHEST)
    node_mass = jnp.einsum("gsn,s->gn", one_hot, scen_weight, precision=lax.Precision.HIGHEST)
    safe_mass = node_mass + (node_mass <= 0.0).astype(jnp.float32)
    average = node_sum / safe_mass[:, :, None]
    spread_back = jnp.einsum("gsn,gnc->sgc", one_hot, average, precision=lax.Precision.HIGHEST)
    multiplier_out = multiplier + PENALTY * (invest - spread_back)
    return (primal, dual_var, invest, multiplier_out)
```

```python
import jax
import jax.numpy as jnp
from jax import lax
from jax.experimental import pallas as pl
from jax.experimental.pallas import tpu as pltpu
from jax.sharding import PartitionSpec as P

ITERS = 8
RAMP_WEIGHT = 0.5
PENALTY = 1.0
STEP_PRIMAL = 0.3
STEP_INVEST = 0.5
STEP_DUAL = 0.3
STEP_CAP = 0.05

MESH = pl.DeviceIdType.MESH
HOURS_LOCAL = 168
HALVES = ((0, 80), (80, 88))
NH = 16
COLS_CORE = 512
COLS = 1024
CONS = 256
PAD = 8
F32 = jnp.float32
BF16 = jnp.bfloat16


def hop_order():
    def hops(d):
        y, z = d % 4, d // 4
        return min(y, 4 - y) + min(z, 4 - z)

    return sorted(range(1, NH), key=lambda d: -hops(d))


def kernel(
    cost_h, icost_h, tile_h, mask_h, dem_h, disp_h, dual_h, cap_h, inv_h, mult_h, cons_h, weight_s, node_s,
    disp_o, dual_o, inv_o, mult_o,
    cost_v, prim_v, a_v, capl_v, tile_v, mask_v, ml_v, m_v, mt_v, pre_v, dem_v,
    xs_v, xr_v, pr_v, p0s_v, p0r_v, he_v, hr_v, edge_v, h0s_v, h0r_v,
    il_v, ic_v, fold_v, frecv_v, invs_v, base_v, sb_v, wn_v, wnr_v, co_v, g_v, tmp_v, do_v,
    load_sem, xsend, xrecv, psend, precv, p0send, p0recv, hsend, hrecv, h0send, h0recv,
    csend, crecv, gsend, grecv, osend, orecv, oload,
):
    s_at, h_at, r_at = lax.axis_index("scen"), lax.axis_index("hour"), lax.axis_index("reg")
    core = lax.rem(r_at, 2)
    other = 1 - core
    r_core = r_at + 1 - 2 * core
    r_chip = lax.rem(r_at + 2, 4)
    y_at, z_at = lax.rem(h_at, 4), lax.div(h_at, 4)

    def hour_rel(d):
        return lax.rem(z_at + d // 4, 4) * 4 + lax.rem(y_at + d % 4, 4)

    order = hop_order()
    left, right = lax.rem(h_at + NH - 1, NH), lax.rem(h_at + 1, NH)
    peer_core = (s_at, h_at, r_core)
    peer_chip = (s_at, h_at, r_chip)
    peer_o0 = (1 - s_at, h_at, r_at)
    peer_o1 = (1 - s_at, h_at, r_core)

    greeted = [(s_at, hour_rel(d), r) for d in order for r in (r_at, r_core)]
    greeted += [peer_core, peer_chip, peer_o0, peer_o1]
    barrier = pltpu.get_barrier_semaphore()
    for peer in greeted:
        pl.semaphore_signal(barrier, inc=1, device_id=peer, device_id_type=MESH)

    own_pair = pl.ds(2 * core, 2)
    oth_pair = pl.ds(2 * other, 2)
    own_cols = pl.ds(pl.multiple_of(core * COLS_CORE, COLS_CORE), COLS_CORE)
    body_rows = pl.ds(PAD, HOURS_LOCAL)

    def load(n, src, dst):
        cp = pltpu.make_async_copy(src, dst, load_sem.at[n])
        cp.start()
        return cp

    c_cap = load(0, cap_h, capl_v)
    c_edge0 = load(1, disp_h.at[:, pl.ds(0, 8), :], edge_v.at[0])
    c_edge1 = load(2, disp_h.at[:, pl.ds(HOURS_LOCAL - 8, 8), :], edge_v.at[1])
    c_tile = load(3, tile_h.at[0], tile_v)
    c_mask = load(4, mask_h.at[0], mask_v)
    c_inv = load(5, inv_h, il_v.at[0])
    c_mult = load(6, mult_h, il_v.at[1])
    c_cons = load(7, cons_h, il_v.at[2])
    c_ic = load(8, icost_h, ic_v)
    c_disp = load(9, disp_h.at[own_pair], prim_v.at[0, :, body_rows, own_cols])
    c_a = load(10, cap_h.at[own_pair], a_v.at[:, :, own_cols])
    c_cost = load(11, cost_h.at[own_pair], cost_v.at[:, :, own_cols])
    c_dual = load(12, dual_h.at[own_pair], pre_v)
    c_dem = load(13, dem_h.at[own_pair], dem_v)

    c_cap.wait()
    for pair in range(2):
        for s in range(2):
            for i in range(4):
                p0s_v[pair, s, i:i + 1, :] = jnp.sum(
                    capl_v[2 * pair + s, :, 128 * i:128 * (i + 1)], axis=0, keepdims=True
                )
    p0r_v[core, h_at] = p0s_v[core]

    c_edge0.wait()
    c_edge1.wait()
    for s in range(4):
        h0s_v[0, s] = edge_v[0, s, 0:1, :]
        h0s_v[1, s] = edge_v[1, s, 7:8, :]

    c_tile.wait()
    c_mask.wait()
    ml_v[...] = tile_v[...] * mask_v[...].astype(BF16)

    c_inv.wait()
    c_mult.wait()
    c_cons.wait()
    c_ic.wait()
    for pair in range(2):
        for s in range(2):
            at = 2 * pair + s
            base = ic_v[...] + il_v[1, at] - PENALTY * il_v[2, at]
            cap0 = il_v[0, at]
            for g in range(3):
                for i in range(4):
                    lanes = slice(128 * i, 128 * (i + 1))
                    fold_v[pair, 0, s, g, i:i + 1, :] = cap0[g:g + 1, lanes]
                    fold_v[pair, 1, s, g, i:i + 1, :] = base[g:g + 1, lanes]

    for s in range(4):
        for g in range(3):
            wn_v[4 * s + g:4 * s + g + 1, :] = jnp.full((1, 128), node_s[g, s].astype(F32), F32)
        wn_v[4 * s + 3:4 * s + 4, :] = jnp.full((1, 128), weight_s[s], F32)

    pl.semaphore_wait(barrier, len(greeted))

    def send(src, dst, ssem, rsem, peer):
        cp = pltpu.make_async_remote_copy(
            src_ref=src, dst_ref=dst, send_sem=ssem, recv_sem=rsem, device_id=peer, device_id_type=MESH
        )
        cp.start()
        return cp

    first = []
    for d in order + [0]:
        for cross in (0, 1):
            if d == 0 and cross == 0:
                continue
            peer = (s_at, hour_rel(d), r_core if cross else r_at)
            first.append(send(
                p0s_v.at[other if cross else core], p0r_v.at[core, h_at],
                p0send.at[cross, d], p0recv.at[cross, d], peer,
            ))
    start_halo = []
    for side, to in ((0, left), (1, right)):
        for cross in (0, 1):
            peer = (s_at, to, r_core if cross else r_at)
            pair = oth_pair if cross else own_pair
            start_halo.append(send(
                h0s_v.at[side, pair], h0r_v.at[1 - side, core],
                h0send.at[side, cross], h0recv.at[side, cross], peer,
            ))
    swaps = [
        send(ml_v, m_v.at[:, own_cols], csend.at[0], crecv.at[0], peer_core),
        send(fold_v.at[other], frecv_v, csend.at[1], crecv.at[1], peer_core),
        send(disp_h.at[oth_pair], prim_v.at[0, :, body_rows, own_cols], csend.at[2], crecv.at[2], peer_core),
        send(cap_h.at[oth_pair], a_v.at[:, :, own_cols], csend.at[3], crecv.at[3], peer_core),
        send(cost_h.at[oth_pair], cost_v.at[:, :, own_cols], csend.at[4], crecv.at[4], peer_core),
    ]
    weights = send(wn_v, wnr_v, csend.at[5], crecv.at[5], peer_o0)
    c_ml = load(14, ml_v, m_v.at[:, own_cols])

    c_ml.wait()
    swaps[0].wait()
    for j in range(4):
        mt_v[256 * j:256 * (j + 1), :] = m_v[:, 256 * j:256 * (j + 1)].T
    swaps[1].wait()
    for s in range(2):
        for g in range(3):
            for n, dest in ((0, invs_v), (1, base_v)):
                mine, its = fold_v[core, n, s, g], frecv_v[n, s, g]
                dest[s, g] = jnp.concatenate(
                    [jnp.where(core == 0, mine, its), jnp.where(core == 0, its, mine)], axis=0
                )
    sb_v[...] = jnp.zeros_like(sb_v)
    weights.wait()

    def row_of(s, g):
        ref = wn_v if s < 4 else wnr_v
        at = 4 * (s % 4) + g
        return ref[at:at + 1, :]

    for g in range(3):
        nodes = [row_of(s, g) for s in range(8)]
        for s in range(4):
            parts = [jnp.where(nodes[t] == nodes[s], row_of(t, 3), 0.0) for t in range(8)]
            mass = ((parts[0] + parts[1]) + (parts[2] + parts[3])) + ((parts[4] + parts[5]) + (parts[6] + parts[7]))
            scale = 1.0 / (mass + jnp.where(mass <= 0.0, 1.0, 0.0))
            for t in range(8):
                at = (3 * s + g) * 8 + t
                co_v[at:at + 1, :] = parts[t] * scale

    for cp in start_halo:
        cp.wait()
    c_disp.wait()
    swaps[2].wait()
    keep_left = jnp.where(h_at > 0, 1.0, 0.0).astype(F32)
    keep_right = jnp.where(h_at < NH - 1, 1.0, 0.0).astype(F32)
    for s in range(2):
        for src in range(2):
            lanes = slice(COLS_CORE * src, COLS_CORE * (src + 1))
            prim_v[0, s, PAD - 1:PAD, lanes] = h0r_v[0, src, s] * keep_left
            prim_v[0, s, PAD + HOURS_LOCAL:PAD + HOURS_LOCAL + 1, lanes] = h0r_v[1, src, s] * keep_right
    c_a.wait()
    swaps[3].wait()
    c_cost.wait()
    swaps[4].wait()
    c_dual.wait()
    c_dem.wait()

    def image_copy(slot, s, half):
        rows = pl.ds(2 * HALVES[half][0], 2 * HALVES[half][1])
        return pltpu.make_async_remote_copy(
            src_ref=xs_v.at[s, rows], dst_ref=xr_v.at[slot, s, rows],
            send_sem=xsend.at[s, half], recv_sem=xrecv.at[slot, s, half],
            device_id=peer_chip, device_id_type=MESH,
        )

    def halo_copy(slot, side, s):
        return pltpu.make_async_remote_copy(
            src_ref=he_v.at[side, s], dst_ref=hr_v.at[slot, 1 - side, s],
            send_sem=hsend.at[side, s], recv_sem=hrecv.at[slot, 1 - side, s],
            device_id=(s_at, left if side == 0 else right, r_at), device_id_type=MESH,
        )

    def sum_copy(slot, d):
        return pltpu.make_async_remote_copy(
            src_ref=pr_v.at[slot, h_at], dst_ref=pr_v.at[slot, h_at],
            send_sem=psend.at[slot, d], recv_sem=precv.at[slot, d],
            device_id=(s_at, hour_rel(d), r_at), device_id_type=MESH,
        )

    def dual_update(last, s, half):
        r0, n = HALVES[half]
        rows = pl.ds(r0, n)
        image_copy(last, s, half).wait_recv()
        got = xr_v[last, s, 2 * r0:2 * (r0 + n), :].astype(F32)
        got = jnp.concatenate([got[:n], got[n:]], axis=1)
        pre_v[s, rows, :] = jnp.maximum(pre_v[s, rows, :] - STEP_DUAL * got, 0.0)

    def chunk(k, now, s, half):
        r0, n = HALVES[half]
        nxt = 1 - now

        @pl.when(k > 0)
        def _():
            dual_update(nxt, s, half)
            side = half
            halo_copy(now, 1 - side, s).wait_recv()
            if half == 0:
                prim_v[now, s, PAD - 1:PAD, :] = hr_v[now, 0, s] * keep_left
            else:
                prim_v[now, s, PAD + HOURS_LOCAL:PAD + HOURS_LOCAL + 1, :] = hr_v[now, 1, s] * keep_right

        dual = pre_v[s, r0:r0 + n, :]
        low = dual.astype(BF16)
        image = None
        for j in range(4):
            cols = slice(256 * j, 256 * (j + 1))
            pulled = jnp.dot(low, m_v[:, cols], preferred_element_type=F32)
            p = prim_v[now, s, PAD + r0:PAD + r0 + n, cols]
            up = prim_v[now, s, PAD + r0 - 1:PAD + r0 + n - 1, cols]
            down = prim_v[now, s, PAD + r0 + 1:PAD + r0 + n + 1, cols]
            sb = jnp.concatenate([sb_v[s, 2 * j:2 * j + 1, :], sb_v[s, 2 * j + 1:2 * j + 2, :]], axis=1)
            cap = jnp.maximum(a_v[s, r0:r0 + n, cols] - sb, 0.0)
            rest = (cost_v[s, r0:r0 + n, cols] - pulled) + cap
            fresh = (
                (1.0 - 2.0 * RAMP_WEIGHT * STEP_PRIMAL) * p
                + (RAMP_WEIGHT * STEP_PRIMAL) * (up + down)
                - STEP_PRIMAL * rest
            )
            fresh = jnp.maximum(fresh, 0.0)
            ext = 2.0 * fresh - p
            prim_v[nxt, s, PAD + r0:PAD + r0 + n, cols] = fresh
            a_v[s, r0:r0 + n, cols] = cap + STEP_CAP * ext
            part = jnp.dot(ext.astype(BF16), mt_v[cols, :], preferred_element_type=F32)
            image = part if image is None else image + part

        @pl.when(k > 0)
        def _():
            image_copy(now, s, half).wait_send()

        xs_v[s, 2 * r0:2 * (r0 + n), :] = jnp.concatenate([image[:, :128], image[:, 128:]], axis=0).astype(BF16)
        image_copy(now, s, half).start()
        pre_v[s, r0:r0 + n, :] = dual + STEP_DUAL * (dem_v[s, r0:r0 + n, :] - image)

        @pl.when(k < ITERS - 1)
        def _():
            side = half

            @pl.when(k > 0)
            def _():
                halo_copy(nxt, side, s).wait_send()

            row = PAD if half == 0 else PAD + HOURS_LOCAL - 1
            he_v[side, s] = prim_v[nxt, s, row:row + 1, :]
            halo_copy(nxt, side, s).start()

    def invest_step(total, s):
        mean = total * (1.0 / (NH * HOURS_LOCAL))
        spent = None
        for g in range(3):
            inv = invs_v[s, g]
            grad = base_v[s, g] + PENALTY * inv - mean
            new = jnp.maximum(inv - STEP_INVEST * grad, 0.0)
            invs_v[s, g] = new
            ext = 2.0 * new - inv
            spent = ext if spent is None else spent + ext
        sb_v[s] = STEP_CAP * spent

    def sums_in(k, now):
        @pl.when(k == 0)
        def _():
            for cp in first:
                cp.wait()
            for s in range(2):
                parts = []
                for src in range(2):
                    total = p0r_v[src, 0, s]
                    for h in range(1, NH):
                        total = total + p0r_v[src, h, s]
                    parts.append(total)
                invest_step(jnp.concatenate(parts, axis=0), s)

        @pl.when(k > 0)
        def _():
            for d in order:
                sum_copy(now, d).wait_send()
            for d in order[::-1]:
                sum_copy(now, d).wait_recv()
            for s in range(2):
                parts = [pr_v[now, h, s] for h in range(NH)]
                while len(parts) > 1:
                    parts = [parts[i] + parts[i + 1] for i in range(0, len(parts), 2)]
                invest_step(parts[0], s)

    def step(k, carry):
        now = lax.rem(k, 2)
        nxt = 1 - now
        for s in range(2):
            for half in range(2):
                chunk(k, now, s, half)
        sums_in(k, now)

        @pl.when(k < ITERS - 1)
        def _():
            for s in range(2):
                for j in range(8):
                    left_over = jnp.maximum(a_v[s, :, 128 * j:128 * (j + 1)] - sb_v[s, j:j + 1, :], 0.0)
                    pr_v[nxt, h_at, s, j:j + 1, :] = jnp.sum(left_over, axis=0, keepdims=True)
            for d in order:
                sum_copy(nxt, d).start()

        @pl.when(k == ITERS - 1)
        def _():
            g_v[0, core] = invs_v[...]

        return carry

    lax.fori_loop(0, ITERS, step, 0)

    gathers = [
        send(g_v.at[0, core], g_v.at[1, core], gsend.at[1], grecv.at[1], peer_o0),
        send(g_v.at[0, core], g_v.at[1, core], gsend.at[2], grecv.at[2], peer_o1),
        send(g_v.at[0, core], g_v.at[0, core], gsend.at[0], grecv.at[0], peer_core),
    ]
    end = ITERS % 2
    outs = [
        send(
            prim_v.at[end, :, body_rows, pl.ds(pl.multiple_of(other * COLS_CORE, COLS_CORE), COLS_CORE)],
            disp_o.at[own_pair], osend.at[0], orecv.at[0], peer_core,
        )
    ]
    c_own = pltpu.make_async_copy(prim_v.at[end, :, body_rows, own_cols], disp_o.at[own_pair], oload.at[0])
    c_own.start()

    on_first = jnp.where(r_at < 2, 1.0, 0.0).astype(F32) > 0.5
    for s in range(2):
        for half in range(2):
            image_copy(1 - end, s, half).wait_send()
            dual_update(1 - end, s, half)
        d = pre_v[s]
        d = jnp.where(on_first, d[:, :128], d[:, 128:])
        lo, hi = d[:, :64], d[:, 64:]
        do_v[0, s] = jnp.where(core == 0, lo, hi)
        do_v[1, s] = jnp.where(core == 0, hi, lo)
    outs.append(send(do_v.at[1], dual_o.at[own_pair], osend.at[1], orecv.at[1], peer_core))
    c_dual_own = pltpu.make_async_copy(do_v.at[0], dual_o.at[own_pair], oload.at[1])
    c_dual_own.start()
    for side in range(2):
        for s in range(2):
            halo_copy(end, side, s).wait_send()

    for cp in gathers[::-1]:
        cp.wait()
    for g in range(3):
        invs = [g_v[t // 4, (t // 2) % 2, t % 2, g] for t in range(8)]
        for s in range(4):
            spread = None
            for t in range(8):
                at = (3 * s + g) * 8 + t
                term = co_v[at:at + 1, :] * invs[t]
                spread = term if spread is None else spread + term
            tmp_v[0, 3 * s + g] = invs[s]
            tmp_v[1, 3 * s + g] = PENALTY * (invs[s] - spread)
    for s in range(4):
        for g in range(3):
            for i in range(4):
                lanes = slice(128 * i, 128 * (i + 1))
                inv_o[s, g:g + 1, lanes] = tmp_v[0, 3 * s + g, pl.ds(4 * core + i, 1), :]
                mult_o[s, g:g + 1, lanes] = il_v[1, s, g:g + 1, lanes] + tmp_v[1, 3 * s + g, pl.ds(4 * core + i, 1), :]
    for cp in outs:
        cp.wait()
    c_own.wait()
    c_dual_own.wait()


def shards(*args):
    hbm = pl.BlockSpec(memory_space=pltpu.HBM)
    vmem = pl.BlockSpec(memory_space=pltpu.VMEM)
    smem = pl.BlockSpec(memory_space=pltpu.SMEM)
    dma = pltpu.SemaphoreType.DMA
    return pl.pallas_call(
        kernel,
        out_shape=(
            jax.ShapeDtypeStruct((4, HOURS_LOCAL, COLS_CORE), F32),
            jax.ShapeDtypeStruct((4, HOURS_LOCAL, 64), F32),
            jax.ShapeDtypeStruct((4, 3, COLS_CORE), F32),
            jax.ShapeDtypeStruct((4, 3, COLS_CORE), F32),
        ),
        in_specs=[hbm] * 11 + [smem] * 2,
        out_specs=(hbm, hbm, vmem, vmem),
        scratch_shapes=[
            pltpu.VMEM((2, HOURS_LOCAL, COLS), F32),
            pltpu.VMEM((2, 2, HOURS_LOCAL + 2 * PAD, COLS), F32),
            pltpu.VMEM((2, HOURS_LOCAL, COLS), F32),
            pltpu.VMEM((4, HOURS_LOCAL, COLS_CORE), F32),
            pltpu.VMEM((CONS, COLS_CORE), BF16),
            pltpu.VMEM((CONS, COLS_CORE), jnp.int32),
            pltpu.VMEM((CONS, COLS_CORE), BF16),
            pltpu.VMEM((CONS, COLS), BF16),
            pltpu.VMEM((COLS, CONS), BF16),
            pltpu.VMEM((2, HOURS_LOCAL, CONS), F32),
            pltpu.VMEM((2, HOURS_LOCAL, CONS), F32),
            pltpu.VMEM((2, 2 * HOURS_LOCAL, 128), BF16),
            pltpu.VMEM((2, 2, 2 * HOURS_LOCAL, 128), BF16),
            pltpu.VMEM((2, NH, 2, 8, 128), F32),
            pltpu.VMEM((2, 2, 4, 128), F32),
            pltpu.VMEM((2, NH, 2, 4, 128), F32),
            pltpu.VMEM((2, 2, 1, COLS), F32),
            pltpu.VMEM((2, 2, 2, 1, COLS), F32),
            pltpu.VMEM((2, 4, 8, COLS_CORE), F32),
            pltpu.VMEM((2, 4, 1, COLS_CORE), F32),
            pltpu.VMEM((2, 2, 2, 1, COLS_CORE), F32),
            pltpu.VMEM((3, 4, 3, COLS_CORE), F32),
            pltpu.VMEM((3, COLS_CORE), F32),
            pltpu.VMEM((2, 2, 2, 3, 4, 128), F32),
            pltpu.VMEM((2, 2, 3, 4, 128), F32),
            pltpu.VMEM((2, 3, 8, 128), F32),
            pltpu.VMEM((2, 3, 8, 128), F32),
            pltpu.VMEM((2, 8, 128), F32),
            pltpu.VMEM((16, 128), F32),
            pltpu.VMEM((16, 128), F32),
            pltpu.VMEM((96, 128), F32),
            pltpu.VMEM((2, 2, 2, 3, 8, 128), F32),
            pltpu.VMEM((2, 12, 8, 128), F32),
            pltpu.VMEM((2, 2, HOURS_LOCAL, 64), F32),
            dma((15,)),
            dma((2, 2)), dma((2, 2, 2)),
            dma((2, NH)), dma((2, NH)),
            dma((2, NH)), dma((2, NH)),
            dma((2, 2)), dma((2, 2, 2)),
            dma((2, 2)), dma((2, 2)),
            dma((6,)), dma((6,)),
            dma((3,)), dma((3,)),
            dma((2,)), dma((2,)), dma((2,)),
        ],
        compiler_params=pltpu.CompilerParams(
            collective_id=0, has_side_effects=True, vmem_limit_bytes=48 * 2**20
        ),
        cost_estimate=pl.CostEstimate(flops=3 * 10**9, bytes_accessed=9 * 10**6, transcendentals=0),
    )(*args)


def solution(mesh):
    placed = (
        P("scen", "hour", "reg"),
        P(None, "reg"),
        P("hour", None, "reg"),
        P("hour", None, "reg"),
        P("scen", "hour", None),
        P("scen", "hour", "reg"),
        P("scen", "hour", None),
        P("scen", "hour", "reg"),
        P("scen", None, "reg"),
        P("scen", None, "reg"),
        P("scen", None, "reg"),
        P("scen"),
        P(None, "scen"),
    )
    return jax.shard_map(
        shards,
        mesh=mesh,
        in_specs=placed,
        out_specs=(
            P("scen", "hour", "reg"),
            P("scen", "hour", "reg"),
            P("scen", None, "reg"),
            P("scen", None, "reg"),
        ),
        check_vma=False,
    )
```

```python
import jax
import jax.numpy as jnp
from jax import lax
from jax.experimental import pallas as pl
from jax.experimental.pallas import tpu as pltpu
from jax.sharding import PartitionSpec as P

ITERS = 8
RAMP_WEIGHT = 0.5
PENALTY = 1.0
STEP_PRIMAL = 0.3
STEP_INVEST = 0.5
STEP_DUAL = 0.3
STEP_CAP = 0.05

MESH = pl.DeviceIdType.MESH
HOURS_LOCAL = 168
HALVES = ((0, 80), (80, 88))
NH = 16
COLS_CORE = 512
COLS = 1024
CONS = 256
PAD = 8
F32 = jnp.float32
BF16 = jnp.bfloat16


def hop_order():
    def hops(d):
        y, z = d % 4, d // 4
        return min(y, 4 - y) + min(z, 4 - z)

    return sorted(range(1, NH), key=lambda d: -hops(d))


def kernel(
    cost_h, icost_h, tile_h, mask_h, dem_h, disp_h, dual_h, cap_h, inv_h, mult_h, cons_h, weight_h, node_h,
    disp_o, dual_o, inv_o, mult_o,
    cost_v, prim_v, a_v, capl_v, tile_v, mask_v, ml_v, m_v, mt_v, pre_v, dem_v,
    xs_v, xr_v, pr_v, p0s_v, p0r_v, he_v, hr_v, edge_v, h0s_v, h0r_v,
    il_v, ic_v, fold_v, frecv_v, invs_v, base_v, sb_v, wn_v, wnr_v, co_v, g_v, tmp_v, do_v, weight_s, node_s,
    load_sem, xsend, xrecv, psend, precv, p0send, p0recv, hsend, hrecv, h0send, h0recv,
    csend, crecv, gsend, grecv, osend, orecv, oload,
):
    s_at, h_at, r_at = lax.axis_index("scen"), lax.axis_index("hour"), lax.axis_index("reg")
    core = lax.rem(r_at, 2)
    other = 1 - core
    r_core = r_at + 1 - 2 * core
    r_chip = lax.rem(r_at + 2, 4)
    y_at, z_at = lax.rem(h_at, 4), lax.div(h_at, 4)

    def hour_rel(d):
        return lax.rem(z_at + d // 4, 4) * 4 + lax.rem(y_at + d % 4, 4)

    order = hop_order()
    left, right = lax.rem(h_at + NH - 1, NH), lax.rem(h_at + 1, NH)
    peer_core = (s_at, h_at, r_core)
    peer_chip = (s_at, h_at, r_chip)
    peer_o0 = (1 - s_at, h_at, r_at)
    peer_o1 = (1 - s_at, h_at, r_core)

    greeted = [(s_at, hour_rel(d), r) for d in order for r in (r_at, r_core)]
    greeted += [peer_core, peer_chip, peer_o0, peer_o1]
    barrier = pltpu.get_barrier_semaphore()
    for peer in greeted:
        pl.semaphore_signal(barrier, inc=1, device_id=peer, device_id_type=MESH)

    own_pair = pl.ds(2 * core, 2)
    oth_pair = pl.ds(2 * other, 2)
    own_cols = pl.ds(pl.multiple_of(core * COLS_CORE, COLS_CORE), COLS_CORE)
    body_rows = pl.ds(PAD, HOURS_LOCAL)

    def load(n, src, dst):
        cp = pltpu.make_async_copy(src, dst, load_sem.at[n])
        cp.start()
        return cp

    c_cap = load(0, cap_h, capl_v)
    c_edge0 = load(1, disp_h.at[:, pl.ds(0, 8), :], edge_v.at[0])
    c_edge1 = load(2, disp_h.at[:, pl.ds(HOURS_LOCAL - 8, 8), :], edge_v.at[1])
    c_tile = load(3, tile_h.at[0], tile_v)
    c_mask = load(4, mask_h.at[0], mask_v)
    c_inv = load(5, inv_h, il_v.at[0])
    c_mult = load(6, mult_h, il_v.at[1])
    c_cons = load(7, cons_h, il_v.at[2])
    c_ic = load(8, icost_h, ic_v)
    c_weight = load(15, weight_h, weight_s)
    c_node = load(16, node_h, node_s)
    c_disp = load(9, disp_h.at[own_pair], prim_v.at[0, :, body_rows, own_cols])
    c_a = load(10, cap_h.at[own_pair], a_v.at[:, :, own_cols])
    c_cost = load(11, cost_h.at[own_pair], cost_v.at[:, :, own_cols])
    c_dual = load(12, dual_h.at[own_pair], pre_v)
    c_dem = load(13, dem_h.at[own_pair], dem_v)

    c_cap.wait()
    for pair in range(2):
        for s in range(2):
            for i in range(4):
                p0s_v[pair, s, i:i + 1, :] = jnp.sum(
                    capl_v[2 * pair + s, :, 128 * i:128 * (i + 1)], axis=0, keepdims=True
                )
    p0r_v[core, h_at] = p0s_v[core]

    c_edge0.wait()
    c_edge1.wait()
    for s in range(4):
        h0s_v[0, s] = edge_v[0, s, 0:1, :]
        h0s_v[1, s] = edge_v[1, s, 7:8, :]

    c_tile.wait()
    c_mask.wait()
    ml_v[...] = tile_v[...] * mask_v[...].astype(BF16)

    c_inv.wait()
    c_mult.wait()
    c_cons.wait()
    c_ic.wait()
    for pair in range(2):
        for s in range(2):
            at = 2 * pair + s
            for g in range(3):
                cap0 = il_v[0, g, at:at + 1, :]
                base = ic_v[g:g + 1, :] + il_v[1, g, at:at + 1, :] - PENALTY * il_v[2, g, at:at + 1, :]
                for i in range(4):
                    lanes = slice(128 * i, 128 * (i + 1))
                    fold_v[pair, 0, s, g, i:i + 1, :] = cap0[:, lanes]
                    fold_v[pair, 1, s, g, i:i + 1, :] = base[:, lanes]

    c_weight.wait()
    c_node.wait()
    for s in range(4):
        for g in range(3):
            wn_v[4 * s + g:4 * s + g + 1, :] = jnp.full((1, 128), node_s[g, s].astype(F32), F32)
        wn_v[4 * s + 3:4 * s + 4, :] = jnp.full((1, 128), weight_s[s], F32)

    pl.semaphore_wait(barrier, len(greeted))

    def send(src, dst, ssem, rsem, peer):
        cp = pltpu.make_async_remote_copy(
            src_ref=src, dst_ref=dst, send_sem=ssem, recv_sem=rsem, device_id=peer, device_id_type=MESH
        )
        cp.start()
        return cp

    first = []
    for d in order + [0]:
        for cross in (0, 1):
            if d == 0 and cross == 0:
                continue
            peer = (s_at, hour_rel(d), r_core if cross else r_at)
            first.append(send(
                p0s_v.at[other if cross else core], p0r_v.at[core, h_at],
                p0send.at[cross, d], p0recv.at[cross, d], peer,
            ))
    start_halo = []
    for side, to in ((0, left), (1, right)):
        for cross in (0, 1):
            peer = (s_at, to, r_core if cross else r_at)
            pair = oth_pair if cross else own_pair
            start_halo.append(send(
                h0s_v.at[side, pair], h0r_v.at[1 - side, core],
                h0send.at[side, cross], h0recv.at[side, cross], peer,
            ))
    swaps = [
        send(ml_v, m_v.at[:, own_cols], csend.at[0], crecv.at[0], peer_core),
        send(fold_v.at[other], frecv_v, csend.at[1], crecv.at[1], peer_core),
        send(disp_h.at[oth_pair], prim_v.at[0, :, body_rows, own_cols], csend.at[2], crecv.at[2], peer_core),
        send(cap_h.at[oth_pair], a_v.at[:, :, own_cols], csend.at[3], crecv.at[3], peer_core),
        send(cost_h.at[oth_pair], cost_v.at[:, :, own_cols], csend.at[4], crecv.at[4], peer_core),
    ]
    weights = send(wn_v, wnr_v, csend.at[5], crecv.at[5], peer_o0)
    c_ml = load(14, ml_v, m_v.at[:, own_cols])

    c_ml.wait()
    swaps[0].wait()
    for j in range(4):
        mt_v[256 * j:256 * (j + 1), :] = m_v[:, 256 * j:256 * (j + 1)].T
    swaps[1].wait()
    for s in range(2):
        for g in range(3):
            for n, dest in ((0, invs_v), (1, base_v)):
                mine, its = fold_v[core, n, s, g], frecv_v[n, s, g]
                dest[s, g] = jnp.concatenate(
                    [jnp.where(core == 0, mine, its), jnp.where(core == 0, its, mine)], axis=0
                )
    sb_v[...] = jnp.zeros_like(sb_v)
    weights.wait()

    def row_of(s, g):
        ref = wn_v if s < 4 else wnr_v
        at = 4 * (s % 4) + g
        return ref[at:at + 1, :]

    for g in range(3):
        nodes = [row_of(s, g) for s in range(8)]
        for s in range(4):
            parts = [jnp.where(nodes[t] == nodes[s], row_of(t, 3), 0.0) for t in range(8)]
            mass = ((parts[0] + parts[1]) + (parts[2] + parts[3])) + ((parts[4] + parts[5]) + (parts[6] + parts[7]))
            scale = 1.0 / (mass + jnp.where(mass <= 0.0, 1.0, 0.0))
            for t in range(8):
                at = (3 * s + g) * 8 + t
                co_v[at:at + 1, :] = parts[t] * scale

    for cp in start_halo:
        cp.wait()
    c_disp.wait()
    swaps[2].wait()
    keep_left = jnp.where(h_at > 0, 1.0, 0.0).astype(F32)
    keep_right = jnp.where(h_at < NH - 1, 1.0, 0.0).astype(F32)
    for s in range(2):
        for src in range(2):
            lanes = slice(COLS_CORE * src, COLS_CORE * (src + 1))
            prim_v[0, s, PAD - 1:PAD, lanes] = h0r_v[0, src, s] * keep_left
            prim_v[0, s, PAD + HOURS_LOCAL:PAD + HOURS_LOCAL + 1, lanes] = h0r_v[1, src, s] * keep_right
    c_a.wait()
    swaps[3].wait()
    c_cost.wait()
    swaps[4].wait()
    c_dual.wait()
    c_dem.wait()

    def image_copy(slot, s, half):
        rows = pl.ds(2 * HALVES[half][0], 2 * HALVES[half][1])
        return pltpu.make_async_remote_copy(
            src_ref=xs_v.at[s, rows], dst_ref=xr_v.at[slot, s, rows],
            send_sem=xsend.at[s, half], recv_sem=xrecv.at[slot, s, half],
            device_id=peer_chip, device_id_type=MESH,
        )

    def halo_copy(slot, side, s):
        return pltpu.make_async_remote_copy(
            src_ref=he_v.at[side, s], dst_ref=hr_v.at[slot, 1 - side, s],
            send_sem=hsend.at[side, s], recv_sem=hrecv.at[slot, 1 - side, s],
            device_id=(s_at, left if side == 0 else right, r_at), device_id_type=MESH,
        )

    def sum_copy(slot, d):
        return pltpu.make_async_remote_copy(
            src_ref=pr_v.at[slot, h_at], dst_ref=pr_v.at[slot, h_at],
            send_sem=psend.at[slot, d], recv_sem=precv.at[slot, d],
            device_id=(s_at, hour_rel(d), r_at), device_id_type=MESH,
        )

    def dual_update(last, s, half):
        r0, n = HALVES[half]
        rows = pl.ds(r0, n)
        image_copy(last, s, half).wait_recv()
        got = xr_v[last, s, 2 * r0:2 * (r0 + n), :].astype(F32)
        got = jnp.concatenate([got[:n], got[n:]], axis=1)
        pre_v[s, rows, :] = jnp.maximum(pre_v[s, rows, :] - STEP_DUAL * got, 0.0)

    def chunk(k, now, s, half):
        r0, n = HALVES[half]
        nxt = 1 - now

        @pl.when(k > 0)
        def _():
            dual_update(nxt, s, half)
            side = half
            halo_copy(now, 1 - side, s).wait_recv()
            if half == 0:
                prim_v[now, s, PAD - 1:PAD, :] = hr_v[now, 0, s] * keep_left
            else:
                prim_v[now, s, PAD + HOURS_LOCAL:PAD + HOURS_LOCAL + 1, :] = hr_v[now, 1, s] * keep_right

        dual = pre_v[s, r0:r0 + n, :]
        low = dual.astype(BF16)
        image = None
        for j in range(4):
            cols = slice(256 * j, 256 * (j + 1))
            pulled = jnp.dot(low, m_v[:, cols], preferred_element_type=F32)
            p = prim_v[now, s, PAD + r0:PAD + r0 + n, cols]
            up = prim_v[now, s, PAD + r0 - 1:PAD + r0 + n - 1, cols]
            down = prim_v[now, s, PAD + r0 + 1:PAD + r0 + n + 1, cols]
            sb = jnp.concatenate([sb_v[s, 2 * j:2 * j + 1, :], sb_v[s, 2 * j + 1:2 * j + 2, :]], axis=1)
            cap = jnp.maximum(a_v[s, r0:r0 + n, cols] - sb, 0.0)
            rest = (cost_v[s, r0:r0 + n, cols] - pulled) + cap
            fresh = (
                (1.0 - 2.0 * RAMP_WEIGHT * STEP_PRIMAL) * p
                + (RAMP_WEIGHT * STEP_PRIMAL) * (up + down)
                - STEP_PRIMAL * rest
            )
            fresh = jnp.maximum(fresh, 0.0)
            ext = 2.0 * fresh - p
            prim_v[nxt, s, PAD + r0:PAD + r0 + n, cols] = fresh
            a_v[s, r0:r0 + n, cols] = cap + STEP_CAP * ext
            part = jnp.dot(ext.astype(BF16), mt_v[cols, :], preferred_element_type=F32)
            image = part if image is None else image + part

        @pl.when(k > 0)
        def _():
            image_copy(now, s, half).wait_send()

        xs_v[s, 2 * r0:2 * (r0 + n), :] = jnp.concatenate([image[:, :128], image[:, 128:]], axis=0).astype(BF16)
        image_copy(now, s, half).start()
        pre_v[s, r0:r0 + n, :] = dual + STEP_DUAL * (dem_v[s, r0:r0 + n, :] - image)

        @pl.when(k < ITERS - 1)
        def _():
            side = half

            @pl.when(k > 0)
            def _():
                halo_copy(nxt, side, s).wait_send()

            row = PAD if half == 0 else PAD + HOURS_LOCAL - 1
            he_v[side, s] = prim_v[nxt, s, row:row + 1, :]
            halo_copy(nxt, side, s).start()

    def invest_step(total, s):
        mean = total * (1.0 / (NH * HOURS_LOCAL))
        spent = None
        for g in range(3):
            inv = invs_v[s, g]
            grad = base_v[s, g] + PENALTY * inv - mean
            new = jnp.maximum(inv - STEP_INVEST * grad, 0.0)
            invs_v[s, g] = new
            ext = 2.0 * new - inv
            spent = ext if spent is None else spent + ext
        sb_v[s] = STEP_CAP * spent

    def sums_in(k, now):
        @pl.when(k == 0)
        def _():
            for cp in first:
                cp.wait()
            for s in range(2):
                parts = []
                for src in range(2):
                    total = p0r_v[src, 0, s]
                    for h in range(1, NH):
                        total = total + p0r_v[src, h, s]
                    parts.append(total)
                invest_step(jnp.concatenate(parts, axis=0), s)

        @pl.when(k > 0)
        def _():
            for d in order:
                sum_copy(now, d).wait_send()
            for d in order[::-1]:
                sum_copy(now, d).wait_recv()
            for s in range(2):
                parts = [pr_v[now, h, s] for h in range(NH)]
                while len(parts) > 1:
                    parts = [parts[i] + parts[i + 1] for i in range(0, len(parts), 2)]
                invest_step(parts[0], s)

    def step(k, carry):
        now = lax.rem(k, 2)
        nxt = 1 - now
        for s in range(2):
            for half in range(2):
                chunk(k, now, s, half)
        sums_in(k, now)

        @pl.when(k < ITERS - 1)
        def _():
            for s in range(2):
                for j in range(8):
                    left_over = jnp.maximum(a_v[s, :, 128 * j:128 * (j + 1)] - sb_v[s, j:j + 1, :], 0.0)
                    pr_v[nxt, h_at, s, j:j + 1, :] = jnp.sum(left_over, axis=0, keepdims=True)
            for d in order:
                sum_copy(nxt, d).start()

        @pl.when(k == ITERS - 1)
        def _():
            g_v[0, core] = invs_v[...]

        return carry

    lax.fori_loop(0, ITERS, step, 0)

    gathers = [
        send(g_v.at[0, core], g_v.at[1, core], gsend.at[1], grecv.at[1], peer_o0),
        send(g_v.at[0, core], g_v.at[1, core], gsend.at[2], grecv.at[2], peer_o1),
        send(g_v.at[0, core], g_v.at[0, core], gsend.at[0], grecv.at[0], peer_core),
    ]
    end = ITERS % 2
    outs = [
        send(
            prim_v.at[end, :, body_rows, pl.ds(pl.multiple_of(other * COLS_CORE, COLS_CORE), COLS_CORE)],
            disp_o.at[own_pair], osend.at[0], orecv.at[0], peer_core,
        )
    ]
    c_own = pltpu.make_async_copy(prim_v.at[end, :, body_rows, own_cols], disp_o.at[own_pair], oload.at[0])
    c_own.start()

    on_first = jnp.where(r_at < 2, 1.0, 0.0).astype(F32) > 0.5
    for s in range(2):
        for half in range(2):
            image_copy(1 - end, s, half).wait_send()
            dual_update(1 - end, s, half)
        d = pre_v[s]
        d = jnp.where(on_first, d[:, :128], d[:, 128:]).T
        lo, hi = d[:64], d[64:]
        do_v[0, s] = jnp.where(core == 0, lo, hi)
        do_v[1, s] = jnp.where(core == 0, hi, lo)
    outs.append(send(do_v.at[1], dual_o.at[own_pair], osend.at[1], orecv.at[1], peer_core))
    c_dual_own = pltpu.make_async_copy(do_v.at[0], dual_o.at[own_pair], oload.at[1])
    c_dual_own.start()
    for side in range(2):
        for s in range(2):
            halo_copy(end, side, s).wait_send()

    for cp in gathers[::-1]:
        cp.wait()
    for g in range(3):
        invs = [g_v[t // 4, (t // 2) % 2, t % 2, g] for t in range(8)]
        for s in range(4):
            spread = None
            for t in range(8):
                at = (3 * s + g) * 8 + t
                term = co_v[at:at + 1, :] * invs[t]
                spread = term if spread is None else spread + term
            tmp_v[0, 3 * s + g] = invs[s]
            tmp_v[1, 3 * s + g] = PENALTY * (invs[s] - spread)
    for s in range(4):
        for g in range(3):
            for i in range(4):
                lanes = slice(128 * i, 128 * (i + 1))
                inv_o[g, s:s + 1, lanes] = tmp_v[0, 3 * s + g, pl.ds(4 * core + i, 1), :]
                mult_o[g, s:s + 1, lanes] = il_v[1, g, s:s + 1, lanes] + tmp_v[1, 3 * s + g, pl.ds(4 * core + i, 1), :]
    for cp in outs:
        cp.wait()
    c_own.wait()
    c_dual_own.wait()


def shards(*args):
    args = args[:8] + tuple(jnp.transpose(x, (1, 0, 2)) for x in args[8:11]) + args[11:]
    hbm = pl.BlockSpec(memory_space=pltpu.HBM)
    vmem = pl.BlockSpec(memory_space=pltpu.VMEM)
    dma = pltpu.SemaphoreType.DMA
    disp, dual, inv, mult = pl.pallas_call(
        kernel,
        out_shape=(
            jax.ShapeDtypeStruct((4, HOURS_LOCAL, COLS_CORE), F32),
            jax.ShapeDtypeStruct((4, 64, HOURS_LOCAL), F32),
            jax.ShapeDtypeStruct((3, 4, COLS_CORE), F32),
            jax.ShapeDtypeStruct((3, 4, COLS_CORE), F32),
        ),
        in_specs=[hbm] * 13,
        out_specs=(hbm, hbm, vmem, vmem),
        scratch_shapes=[
            pltpu.VMEM((2, HOURS_LOCAL, COLS), F32),
            pltpu.VMEM((2, 2, HOURS_LOCAL + 2 * PAD, COLS), F32),
            pltpu.VMEM((2, HOURS_LOCAL, COLS), F32),
            pltpu.VMEM((4, HOURS_LOCAL, COLS_CORE), F32),
            pltpu.VMEM((CONS, COLS_CORE), BF16),
            pltpu.VMEM((CONS, COLS_CORE), jnp.int32),
            pltpu.VMEM((CONS, COLS_CORE), BF16),
            pltpu.VMEM((CONS, COLS), BF16),
            pltpu.VMEM((COLS, CONS), BF16),
            pltpu.VMEM((2, HOURS_LOCAL, CONS), F32),
            pltpu.VMEM((2, HOURS_LOCAL, CONS), F32),
            pltpu.VMEM((2, 2 * HOURS_LOCAL, 128), BF16),
            pltpu.VMEM((2, 2, 2 * HOURS_LOCAL, 128), BF16),
            pltpu.VMEM((2, NH, 2, 8, 128), F32),
            pltpu.VMEM((2, 2, 4, 128), F32),
            pltpu.VMEM((2, NH, 2, 4, 128), F32),
            pltpu.VMEM((2, 2, 1, COLS), F32),
            pltpu.VMEM((2, 2, 2, 1, COLS), F32),
            pltpu.VMEM((2, 4, 8, COLS_CORE), F32),
            pltpu.VMEM((2, 4, 1, COLS_CORE), F32),
            pltpu.VMEM((2, 2, 2, 1, COLS_CORE), F32),
            pltpu.VMEM((3, 3, 4, COLS_CORE), F32),
            pltpu.VMEM((3, COLS_CORE), F32),
            pltpu.VMEM((2, 2, 2, 3, 4, 128), F32),
            pltpu.VMEM((2, 2, 3, 4, 128), F32),
            pltpu.VMEM((2, 3, 8, 128), F32),
            pltpu.VMEM((2, 3, 8, 128), F32),
            pltpu.VMEM((2, 8, 128), F32),
            pltpu.VMEM((16, 128), F32),
            pltpu.VMEM((16, 128), F32),
            pltpu.VMEM((96, 128), F32),
            pltpu.VMEM((2, 2, 2, 3, 8, 128), F32),
            pltpu.VMEM((2, 12, 8, 128), F32),
            pltpu.VMEM((2, 2, 64, HOURS_LOCAL), F32),
            pltpu.SMEM((4,), F32),
            pltpu.SMEM((3, 4), jnp.int32),
            dma((17,)),
            dma((2, 2)), dma((2, 2, 2)),
            dma((2, NH)), dma((2, NH)),
            dma((2, NH)), dma((2, NH)),
            dma((2, 2)), dma((2, 2, 2)),
            dma((2, 2)), dma((2, 2)),
            dma((6,)), dma((6,)),
            dma((3,)), dma((3,)),
            dma((2,)), dma((2,)), dma((2,)),
        ],
        compiler_params=pltpu.CompilerParams(
            collective_id=0, has_side_effects=True, vmem_limit_bytes=58 * 2**20
        ),
        cost_estimate=pl.CostEstimate(flops=3 * 10**9, bytes_accessed=9 * 10**6, transcendentals=0),
    )(*args)
    return disp, jnp.transpose(dual, (0, 2, 1)), jnp.transpose(inv, (1, 0, 2)), jnp.transpose(mult, (1, 0, 2))


def solution(mesh):
    placed = (
        P("scen", "hour", "reg"),
        P(None, "reg"),
        P("hour", None, "reg"),
        P("hour", None, "reg"),
        P("scen", "hour", None),
        P("scen", "hour", "reg"),
        P("scen", "hour", None),
        P("scen", "hour", "reg"),
        P("scen", None, "reg"),
        P("scen", None, "reg"),
        P("scen", None, "reg"),
        P("scen"),
        P(None, "scen"),
    )
    return jax.shard_map(
        shards,
        mesh=mesh,
        in_specs=placed,
        out_specs=(
            P("scen", "hour", "reg"),
            P("scen", "hour", "reg"),
            P("scen", None, "reg"),
            P("scen", None, "reg"),
        ),
        check_vma=False,
    )
```

```python
import jax
import jax.numpy as jnp
from jax import lax
from jax.experimental import pallas as pl
from jax.experimental.pallas import tpu as pltpu
from jax.sharding import PartitionSpec as P

ITERS = 8
RAMP_WEIGHT = 0.5
PENALTY = 1.0
STEP_PRIMAL = 0.3
STEP_INVEST = 0.5
STEP_DUAL = 0.3
STEP_CAP = 0.05

MESH = pl.DeviceIdType.MESH
HOURS_LOCAL = 168
PARTS = (((0, 40), (128, 40)), ((40, 88),))
SENT = ((0, 160), (160, 176))
NH = 16
COLS_CORE = 512
COLS = 1024
CONS = 256
PAD = 8
F32 = jnp.float32
BF16 = jnp.bfloat16


def hop_order():
    def hops(d):
        y, z = d % 4, d // 4
        return min(y, 4 - y) + min(z, 4 - z)

    return sorted(range(1, NH), key=lambda d: -hops(d))


def kernel(
    cost_h, icost_h, tile_h, mask_h, dem_h, disp_h, dual_h, cap_h, inv_h, mult_h, cons_h, weight_h, node_h,
    disp_o, dual_o, inv_o, mult_o,
    cost_v, prim_v, a_v, capl_v, tile_v, mask_v, ml_v, m_v, mt_v, pre_v, dem_v,
    xs_v, xr_v, pr_v, p0s_v, p0r_v, he_v, hr_v, edge_v, h0s_v, h0r_v,
    il_v, ic_v, fold_v, frecv_v, invs_v, base_v, sb_v, wn_v, wnr_v, co_v, g_v, tmp_v, do_v, sum_v, weight_s, node_s,
    load_sem, xsend, xrecv, psend, precv, p0send, p0recv, hsend, hrecv, h0send, h0recv,
    csend, crecv, gsend, grecv, osend, orecv, oload,
):
    s_at, h_at, r_at = lax.axis_index("scen"), lax.axis_index("hour"), lax.axis_index("reg")
    core = lax.rem(r_at, 2)
    other = 1 - core
    r_core = r_at + 1 - 2 * core
    r_chip = lax.rem(r_at + 2, 4)
    y_at, z_at = lax.rem(h_at, 4), lax.div(h_at, 4)

    def hour_rel(d):
        return lax.rem(z_at + d // 4, 4) * 4 + lax.rem(y_at + d % 4, 4)

    order = hop_order()
    left, right = lax.rem(h_at + NH - 1, NH), lax.rem(h_at + 1, NH)
    peer_core = (s_at, h_at, r_core)
    peer_chip = (s_at, h_at, r_chip)
    peer_o0 = (1 - s_at, h_at, r_at)
    peer_o1 = (1 - s_at, h_at, r_core)

    greeted = [(s_at, hour_rel(d), r) for d in order for r in (r_at, r_core)]
    greeted += [peer_core, peer_chip, peer_o0, peer_o1]
    barrier = pltpu.get_barrier_semaphore()
    for peer in greeted:
        pl.semaphore_signal(barrier, inc=1, device_id=peer, device_id_type=MESH)

    own_pair = pl.ds(2 * core, 2)
    oth_pair = pl.ds(2 * other, 2)
    own_cols = pl.ds(pl.multiple_of(core * COLS_CORE, COLS_CORE), COLS_CORE)
    body_rows = pl.ds(PAD, HOURS_LOCAL)

    def load(n, src, dst):
        cp = pltpu.make_async_copy(src, dst, load_sem.at[n])
        cp.start()
        return cp

    c_cap = load(0, cap_h, capl_v)
    c_edge0 = load(1, disp_h.at[:, pl.ds(0, 8), :], edge_v.at[0])
    c_edge1 = load(2, disp_h.at[:, pl.ds(HOURS_LOCAL - 8, 8), :], edge_v.at[1])
    c_tile = load(3, tile_h.at[0], tile_v)
    c_mask = load(4, mask_h.at[0], mask_v)
    c_inv = load(5, inv_h, il_v.at[0])
    c_mult = load(6, mult_h, il_v.at[1])
    c_cons = load(7, cons_h, il_v.at[2])
    c_ic = load(8, icost_h, ic_v)
    c_weight = load(15, weight_h, weight_s)
    c_node = load(16, node_h, node_s)
    c_disp = load(9, disp_h.at[own_pair], prim_v.at[0, :, body_rows, own_cols])
    c_a = load(10, cap_h.at[own_pair], a_v.at[:, :, own_cols])
    c_cost = load(11, cost_h.at[own_pair], cost_v.at[:, :, own_cols])
    c_dual = load(12, dual_h.at[own_pair], pre_v)
    c_dem = load(13, dem_h.at[own_pair], dem_v)

    c_cap.wait()
    for pair in range(2):
        for s in range(2):
            for i in range(4):
                p0s_v[pair, s, i:i + 1, :] = jnp.sum(
                    capl_v[2 * pair + s, :, 128 * i:128 * (i + 1)], axis=0, keepdims=True
                )
    p0r_v[core, h_at] = p0s_v[core]

    c_edge0.wait()
    c_edge1.wait()
    for s in range(4):
        h0s_v[0, s] = edge_v[0, s, 0:1, :]
        h0s_v[1, s] = edge_v[1, s, 7:8, :]

    c_tile.wait()
    c_mask.wait()
    ml_v[...] = tile_v[...] * mask_v[...].astype(BF16)

    c_inv.wait()
    c_mult.wait()
    c_cons.wait()
    c_ic.wait()
    for pair in range(2):
        for s in range(2):
            at = 2 * pair + s
            for g in range(3):
                cap0 = il_v[0, g, at:at + 1, :]
                base = ic_v[g:g + 1, :] + il_v[1, g, at:at + 1, :] - PENALTY * il_v[2, g, at:at + 1, :]
                for i in range(4):
                    lanes = slice(128 * i, 128 * (i + 1))
                    fold_v[pair, 0, s, g, i:i + 1, :] = cap0[:, lanes]
                    fold_v[pair, 1, s, g, i:i + 1, :] = base[:, lanes]

    c_weight.wait()
    c_node.wait()
    for s in range(4):
        for g in range(3):
            wn_v[4 * s + g:4 * s + g + 1, :] = jnp.full((1, 128), node_s[g, s].astype(F32), F32)
        wn_v[4 * s + 3:4 * s + 4, :] = jnp.full((1, 128), weight_s[s], F32)

    pl.semaphore_wait(barrier, len(greeted))

    def send(src, dst, ssem, rsem, peer):
        cp = pltpu.make_async_remote_copy(
            src_ref=src, dst_ref=dst, send_sem=ssem, recv_sem=rsem, device_id=peer, device_id_type=MESH
        )
        cp.start()
        return cp

    def swap(n, s):
        return [
            send(disp_h.at[2 * other + s], prim_v.at[0, s, body_rows, own_cols], csend.at[n], crecv.at[n], peer_core),
            send(cap_h.at[2 * other + s], a_v.at[s, :, own_cols], csend.at[n + 1], crecv.at[n + 1], peer_core),
            send(cost_h.at[2 * other + s], cost_v.at[s, :, own_cols], csend.at[n + 2], crecv.at[n + 2], peer_core),
        ]

    first = []
    for d in order + [0]:
        for cross in (0, 1):
            if d == 0 and cross == 0:
                continue
            peer = (s_at, hour_rel(d), r_core if cross else r_at)
            first.append(send(
                p0s_v.at[other if cross else core], p0r_v.at[core, h_at],
                p0send.at[cross, d], p0recv.at[cross, d], peer,
            ))
        if d == order[0]:
            swap_m = send(ml_v, m_v.at[:, own_cols], csend.at[0], crecv.at[0], peer_core)
            swap_s = [swap(2, 0)]
    start_halo = []
    for side, to in ((0, left), (1, right)):
        for cross in (0, 1):
            peer = (s_at, to, r_core if cross else r_at)
            pair = oth_pair if cross else own_pair
            start_halo.append(send(
                h0s_v.at[side, pair], h0r_v.at[1 - side, core],
                h0send.at[side, cross], h0recv.at[side, cross], peer,
            ))
    swap_s.append(swap(5, 1))
    swap_f = send(fold_v.at[other], frecv_v, csend.at[1], crecv.at[1], peer_core)
    weights = send(wn_v, wnr_v, csend.at[8], crecv.at[8], peer_o0)
    c_ml = load(14, ml_v, m_v.at[:, own_cols])

    sb_v[...] = jnp.zeros_like(sb_v)
    c_ml.wait()
    swap_m.wait()
    for j in range(4):
        mt_v[256 * j:256 * (j + 1), :] = m_v[:, 256 * j:256 * (j + 1)].T
    keep_left = jnp.where(h_at > 0, 1.0, 0.0).astype(F32)
    keep_right = jnp.where(h_at < NH - 1, 1.0, 0.0).astype(F32)
    c_disp.wait()
    c_a.wait()
    c_cost.wait()
    c_dual.wait()
    c_dem.wait()

    def prepare():
        swap_f.wait()
        for s in range(2):
            for g in range(3):
                for n, dest in ((0, invs_v), (1, base_v)):
                    mine, its = fold_v[core, n, s, g], frecv_v[n, s, g]
                    dest[s, g] = jnp.concatenate(
                        [jnp.where(core == 0, mine, its), jnp.where(core == 0, its, mine)], axis=0
                    )

    def coefficients():
        weights.wait()

        def row_of(s, g):
            ref = wn_v if s < 4 else wnr_v
            at = 4 * (s % 4) + g
            return ref[at:at + 1, :]

        for g in range(3):
            nodes = [row_of(s, g) for s in range(8)]
            for s in range(4):
                parts = [jnp.where(nodes[t] == nodes[s], row_of(t, 3), 0.0) for t in range(8)]
                mass = ((parts[0] + parts[1]) + (parts[2] + parts[3])) + ((parts[4] + parts[5]) + (parts[6] + parts[7]))
                scale = 1.0 / (mass + jnp.where(mass <= 0.0, 1.0, 0.0))
                for t in range(8):
                    at = (3 * s + g) * 8 + t
                    co_v[at:at + 1, :] = parts[t] * scale

    def image_copy(slot, s, half):
        rows = pl.ds(*SENT[half])
        return pltpu.make_async_remote_copy(
            src_ref=xs_v.at[s, rows], dst_ref=xr_v.at[slot, s, rows],
            send_sem=xsend.at[s, half], recv_sem=xrecv.at[slot, s, half],
            device_id=peer_chip, device_id_type=MESH,
        )

    def halo_copy(slot, side, s):
        return pltpu.make_async_remote_copy(
            src_ref=he_v.at[side, s], dst_ref=hr_v.at[slot, 1 - side, s],
            send_sem=hsend.at[side, s], recv_sem=hrecv.at[slot, 1 - side, s],
            device_id=(s_at, left if side == 0 else right, r_at), device_id_type=MESH,
        )

    def sum_copy(slot, d):
        return pltpu.make_async_remote_copy(
            src_ref=pr_v.at[slot, h_at], dst_ref=pr_v.at[slot, h_at],
            send_sem=psend.at[slot, d], recv_sem=precv.at[slot, d],
            device_id=(s_at, hour_rel(d), r_at), device_id_type=MESH,
        )

    def rows_of(ref, s, half, cols=slice(None)):
        parts = [ref[s, r0:r0 + n, cols] for r0, n in PARTS[half]]
        return parts[0] if len(parts) == 1 else jnp.concatenate(parts, axis=0)

    def put_rows(ref, s, half, value):
        at = 0
        for r0, n in PARTS[half]:
            ref[s, r0:r0 + n, :] = value[at:at + n]
            at += n

    def dual_update(last, s, half):
        image_copy(last, s, half).wait_recv()
        at, m = SENT[half]
        got = xr_v[last, s, at:at + m, :].astype(F32)
        got = jnp.concatenate([got[:m // 2], got[m // 2:]], axis=1)
        put_rows(pre_v, s, half, jnp.maximum(rows_of(pre_v, s, half) - STEP_DUAL * got, 0.0))

    def chunk(k, now, s, half):
        nxt = 1 - now

        @pl.when(k > 0)
        def _():
            dual_update(nxt, s, half)

        if half == 0:
            @pl.when(k > 0)
            def _():
                for side in range(2):
                    halo_copy(now, side, s).wait_recv()
                prim_v[now, s, PAD - 1:PAD, :] = hr_v[now, 0, s] * keep_left
                prim_v[now, s, PAD + HOURS_LOCAL:PAD + HOURS_LOCAL + 1, :] = hr_v[now, 1, s] * keep_right

            @pl.when(k == 0)
            def _():
                if s == 0:
                    for cp in start_halo:
                        cp.wait()
                for src in range(2):
                    lanes = slice(COLS_CORE * src, COLS_CORE * (src + 1))
                    prim_v[0, s, PAD - 1:PAD, lanes] = h0r_v[0, src, s] * keep_left
                    prim_v[0, s, PAD + HOURS_LOCAL:PAD + HOURS_LOCAL + 1, lanes] = h0r_v[1, src, s] * keep_right
        else:
            @pl.when(k == 0)
            def _():
                for cp in swap_s[s]:
                    cp.wait()

        dual = rows_of(pre_v, s, half)
        low = dual.astype(BF16)
        image = None
        for j in range(4):
            cols = slice(256 * j, 256 * (j + 1))
            pulled_all = jnp.dot(low, m_v[:, cols], preferred_element_type=F32)
            sb = jnp.concatenate([sb_v[s, 2 * j:2 * j + 1, :], sb_v[s, 2 * j + 1:2 * j + 2, :]], axis=1)
            exts = []
            at = 0
            for r0, n in PARTS[half]:
                pulled = pulled_all[at:at + n]
                at += n
                p = prim_v[now, s, PAD + r0:PAD + r0 + n, cols]
                up = prim_v[now, s, PAD + r0 - 1:PAD + r0 + n - 1, cols]
                down = prim_v[now, s, PAD + r0 + 1:PAD + r0 + n + 1, cols]
                cap = jnp.maximum(a_v[s, r0:r0 + n, cols] - sb, 0.0)
                rest = (cost_v[s, r0:r0 + n, cols] - pulled) + cap
                fresh = (
                    (1.0 - 2.0 * RAMP_WEIGHT * STEP_PRIMAL) * p
                    + (RAMP_WEIGHT * STEP_PRIMAL) * (up + down)
                    - STEP_PRIMAL * rest
                )
                fresh = jnp.maximum(fresh, 0.0)
                ext = 2.0 * fresh - p
                prim_v[nxt, s, PAD + r0:PAD + r0 + n, cols] = fresh
                a_v[s, r0:r0 + n, cols] = cap + STEP_CAP * ext
                exts.append(ext)
            ext_all = exts[0] if len(exts) == 1 else jnp.concatenate(exts, axis=0)
            part = jnp.dot(ext_all.astype(BF16), mt_v[cols, :], preferred_element_type=F32)
            image = part if image is None else image + part

        if half == 0:
            @pl.when(k < ITERS - 1)
            def _():
                for side, row in ((0, PAD), (1, PAD + HOURS_LOCAL - 1)):
                    @pl.when(k > 0)
                    def _():
                        halo_copy(nxt, side, s).wait_send()

                    he_v[side, s] = prim_v[nxt, s, row:row + 1, :]
                    halo_copy(nxt, side, s).start()

        @pl.when(k > 0)
        def _():
            image_copy(now, s, half).wait_send()

        at, m = SENT[half]
        xs_v[s, at:at + m, :] = jnp.concatenate([image[:, :128], image[:, 128:]], axis=0).astype(BF16)
        image_copy(now, s, half).start()
        put_rows(pre_v, s, half, dual + STEP_DUAL * (rows_of(dem_v, s, half) - image))

    def invest_step(total, s):
        mean = total * (1.0 / (NH * HOURS_LOCAL))
        spent = None
        for g in range(3):
            inv = invs_v[s, g]
            grad = base_v[s, g] + PENALTY * inv - mean
            new = jnp.maximum(inv - STEP_INVEST * grad, 0.0)
            invs_v[s, g] = new
            ext = 2.0 * new - inv
            spent = ext if spent is None else spent + ext
        sb_v[s] = STEP_CAP * spent

    def sums_in(k, now):
        @pl.when(k == 0)
        def _():
            prepare()
            for cp in first:
                cp.wait()
            for s in range(2):
                parts = []
                for src in range(2):
                    total = p0r_v[src, 0, s]
                    for h in range(1, NH):
                        total = total + p0r_v[src, h, s]
                    parts.append(total)
                invest_step(jnp.concatenate(parts, axis=0), s)

        @pl.when(k > 0)
        def _():
            for d in order[::-1]:
                sum_copy(now, d).wait_recv()
            parts = [pr_v[now, h].astype(F32) for h in range(NH)]
            while len(parts) > 1:
                parts = [parts[i] + parts[i + 1] for i in range(0, len(parts), 2)]
            for s in range(2):
                invest_step(parts[0][8 * s:8 * (s + 1)], s)

    def step(k, carry):
        now = lax.rem(k, 2)
        nxt = 1 - now
        for s in range(2):
            for half in (1, 0):
                chunk(k, now, s, half)
        sums_in(k, now)

        @pl.when(k < ITERS - 1)
        def _():
            for s in range(2):
                for j in range(8):
                    left_over = jnp.maximum(a_v[s, :, 128 * j:128 * (j + 1)] - sb_v[s, j:j + 1, :], 0.0)
                    at = 8 * s + j
                    sum_v[at:at + 1, :] = jnp.sum(left_over, axis=0, keepdims=True)
            pr_v[nxt, h_at] = sum_v[...].astype(BF16)
            for d in order:
                sum_copy(nxt, d).start()

        @pl.when(k > 0)
        def _():
            for d in order:
                sum_copy(now, d).wait_send()

        @pl.when(k == 0)
        def _():
            coefficients()

        @pl.when(k == ITERS - 1)
        def _():
            g_v[0, core] = invs_v[...]

        return carry

    lax.fori_loop(0, ITERS, step, 0)

    gathers = [
        send(g_v.at[0, core], g_v.at[1, core], gsend.at[1], grecv.at[1], peer_o0),
        send(g_v.at[0, core], g_v.at[1, core], gsend.at[2], grecv.at[2], peer_o1),
        send(g_v.at[0, core], g_v.at[0, core], gsend.at[0], grecv.at[0], peer_core),
    ]
    end = ITERS % 2
    outs = [
        send(
            prim_v.at[end, :, body_rows, pl.ds(pl.multiple_of(other * COLS_CORE, COLS_CORE), COLS_CORE)],
            disp_o.at[own_pair], osend.at[0], orecv.at[0], peer_core,
        )
    ]
    c_own = pltpu.make_async_copy(prim_v.at[end, :, body_rows, own_cols], disp_o.at[own_pair], oload.at[0])
    c_own.start()

    on_first = jnp.where(r_at < 2, 1.0, 0.0).astype(F32) > 0.5
    for s in range(2):
        for half in range(2):
            image_copy(1 - end, s, half).wait_send()
            dual_update(1 - end, s, half)
        d = pre_v[s]
        d = jnp.where(on_first, d[:, :128], d[:, 128:]).T
        lo, hi = d[:64], d[64:]
        do_v[0, s] = jnp.where(core == 0, lo, hi)
        do_v[1, s] = jnp.where(core == 0, hi, lo)
    outs.append(send(do_v.at[1], dual_o.at[own_pair], osend.at[1], orecv.at[1], peer_core))
    c_dual_own = pltpu.make_async_copy(do_v.at[0], dual_o.at[own_pair], oload.at[1])
    c_dual_own.start()
    for side in range(2):
        for s in range(2):
            halo_copy(end, side, s).wait_send()

    for cp in gathers[::-1]:
        cp.wait()
    for g in range(3):
        invs = [g_v[t // 4, (t // 2) % 2, t % 2, g] for t in range(8)]
        for s in range(4):
            spread = None
            for t in range(8):
                at = (3 * s + g) * 8 + t
                term = co_v[at:at + 1, :] * invs[t]
                spread = term if spread is None else spread + term
            tmp_v[0, 3 * s + g] = invs[s]
            tmp_v[1, 3 * s + g] = PENALTY * (invs[s] - spread)
    for s in range(4):
        for g in range(3):
            for i in range(4):
                lanes = slice(128 * i, 128 * (i + 1))
                inv_o[g, s:s + 1, lanes] = tmp_v[0, 3 * s + g, pl.ds(4 * core + i, 1), :]
                mult_o[g, s:s + 1, lanes] = il_v[1, g, s:s + 1, lanes] + tmp_v[1, 3 * s + g, pl.ds(4 * core + i, 1), :]
    for cp in outs:
        cp.wait()
    c_own.wait()
    c_dual_own.wait()


def hand_over(disp_i, dual_i, inv_i, mult_i, disp_o, dual_o, inv_o, mult_o, sem):
    copies = []
    pairs = [(inv_i, inv_o), (mult_i, mult_o)]
    for s in range(4):
        pairs.append((disp_i.at[s], disp_o.at[s]))
    pairs.append((dual_i, dual_o))
    for n, (src, dst) in enumerate(pairs):
        copies.append(pltpu.make_async_copy(src, dst, sem.at[n]))
    for cp in copies:
        cp.start()
    for cp in copies:
        cp.wait()


def shards(*args):
    args = args[:8] + tuple(jnp.transpose(x, (1, 0, 2)) for x in args[8:11]) + args[11:]
    hbm = pl.BlockSpec(memory_space=pltpu.HBM)
    vmem = pl.BlockSpec(memory_space=pltpu.VMEM)
    dma = pltpu.SemaphoreType.DMA
    disp, dual, inv, mult = pl.pallas_call(
        kernel,
        out_shape=(
            pltpu.VMEM((4, HOURS_LOCAL, COLS_CORE), F32),
            pltpu.VMEM((4, 64, HOURS_LOCAL), F32),
            pltpu.VMEM((3, 4, COLS_CORE), F32),
            pltpu.VMEM((3, 4, COLS_CORE), F32),
        ),
        in_specs=[hbm] * 13,
        out_specs=(vmem,) * 4,
        scratch_shapes=[
            pltpu.VMEM((2, HOURS_LOCAL, COLS), F32),
            pltpu.VMEM((2, 2, HOURS_LOCAL + 2 * PAD, COLS), F32),
            pltpu.VMEM((2, HOURS_LOCAL, COLS), F32),
            pltpu.VMEM((4, HOURS_LOCAL, COLS_CORE), F32),
            pltpu.VMEM((CONS, COLS_CORE), BF16),
            pltpu.VMEM((CONS, COLS_CORE), jnp.int32),
            pltpu.VMEM((CONS, COLS_CORE), BF16),
            pltpu.VMEM((CONS, COLS), BF16),
            pltpu.VMEM((COLS, CONS), BF16),
            pltpu.VMEM((2, HOURS_LOCAL, CONS), F32),
            pltpu.VMEM((2, HOURS_LOCAL, CONS), F32),
            pltpu.VMEM((2, 2 * HOURS_LOCAL, 128), BF16),
            pltpu.VMEM((2, 2, 2 * HOURS_LOCAL, 128), BF16),
            pltpu.VMEM((2, NH, 16, 128), BF16),
            pltpu.VMEM((2, 2, 4, 128), F32),
            pltpu.VMEM((2, NH, 2, 4, 128), F32),
            pltpu.VMEM((2, 2, 1, COLS), F32),
            pltpu.VMEM((2, 2, 2, 1, COLS), F32),
            pltpu.VMEM((2, 4, 8, COLS_CORE), F32),
            pltpu.VMEM((2, 4, 1, COLS_CORE), F32),
            pltpu.VMEM((2, 2, 2, 1, COLS_CORE), F32),
            pltpu.VMEM((3, 3, 4, COLS_CORE), F32),
            pltpu.VMEM((3, COLS_CORE), F32),
            pltpu.VMEM((2, 2, 2, 3, 4, 128), F32),
            pltpu.VMEM((2, 2, 3, 4, 128), F32),
            pltpu.VMEM((2, 3, 8, 128), F32),
            pltpu.VMEM((2, 3, 8, 128), F32),
            pltpu.VMEM((2, 8, 128), F32),
            pltpu.VMEM((16, 128), F32),
            pltpu.VMEM((16, 128), F32),
            pltpu.VMEM((96, 128), F32),
            pltpu.VMEM((2, 2, 2, 3, 8, 128), F32),
            pltpu.VMEM((2, 12, 8, 128), F32),
            pltpu.VMEM((2, 2, 64, HOURS_LOCAL), F32),
            pltpu.VMEM((16, 128), F32),
            pltpu.SMEM((4,), F32),
            pltpu.SMEM((3, 4), jnp.int32),
            dma((17,)),
            dma((2, 2)), dma((2, 2, 2)),
            dma((2, NH)), dma((2, NH)),
            dma((2, NH)), dma((2, NH)),
            dma((2, 2)), dma((2, 2, 2)),
            dma((2, 2)), dma((2, 2)),
            dma((9,)), dma((9,)),
            dma((3,)), dma((3,)),
            dma((2,)), dma((2,)), dma((2,)),
        ],
        compiler_params=pltpu.CompilerParams(
            collective_id=0, has_side_effects=True, vmem_limit_bytes=58 * 2**20
        ),
        cost_estimate=pl.CostEstimate(flops=3 * 10**9, bytes_accessed=9 * 10**6, transcendentals=0),
    )(*args)
    disp, dual, inv, mult = pl.pallas_call(
        hand_over,
        out_shape=tuple(jax.ShapeDtypeStruct(x.shape, x.dtype) for x in (disp, dual, inv, mult)),
        in_specs=[vmem] * 4,
        out_specs=(hbm,) * 4,
        scratch_shapes=[dma((7,))],
        compiler_params=pltpu.CompilerParams(vmem_limit_bytes=2**20),
        cost_estimate=pl.CostEstimate(flops=0, bytes_accessed=3 * 10**6, transcendentals=0),
    )(disp, dual, inv, mult)
    return disp, jnp.transpose(dual, (0, 2, 1)), jnp.transpose(inv, (1, 0, 2)), jnp.transpose(mult, (1, 0, 2))


def solution(mesh):
    placed = (
        P("scen", "hour", "reg"),
        P(None, "reg"),
        P("hour", None, "reg"),
        P("hour", None, "reg"),
        P("scen", "hour", None),
        P("scen", "hour", "reg"),
        P("scen", "hour", None),
        P("scen", "hour", "reg"),
        P("scen", None, "reg"),
        P("scen", None, "reg"),
        P("scen", None, "reg"),
        P("scen"),
        P(None, "scen"),
    )
    return jax.shard_map(
        shards,
        mesh=mesh,
        in_specs=placed,
        out_specs=(
            P("scen", "hour", "reg"),
            P("scen", "hour", "reg"),
            P("scen", None, "reg"),
            P("scen", None, "reg"),
        ),
        check_vma=False,
    )
```

```python
import jax
import jax.numpy as jnp
from jax import lax
from jax.experimental import pallas as pl
from jax.experimental.pallas import tpu as pltpu
from jax.sharding import PartitionSpec as P

ITERS = 8
RAMP_WEIGHT = 0.5
PENALTY = 1.0
STEP_PRIMAL = 0.3
STEP_INVEST = 0.5
STEP_DUAL = 0.3
STEP_CAP = 0.05

MESH = pl.DeviceIdType.MESH
HOURS_LOCAL = 168
PARTS = (((0, 40), (128, 40)), ((40, 88),))
SENT = ((0, 160), (160, 176))
NH = 16
COLS_CORE = 512
COLS = 1024
CONS = 256
PAD = 8
F32 = jnp.float32
BF16 = jnp.bfloat16


def hop_order():
    def hops(d):
        y, z = d % 4, d // 4
        return min(y, 4 - y) + min(z, 4 - z)

    return sorted(range(1, NH), key=lambda d: -hops(d))


def kernel(
    cost_h, icost_h, tile_h, mask_h, dem_h, disp_h, dual_h, cap_h, inv_h, mult_h, cons_h, weight_h, node_h,
    disp_o, dual_o, inv_o, mult_o,
    cost_v, prim_v, a_v, capl_v, tile_v, mask_v, ml_v, m_v, mt_v, pre_v, dem_v,
    xs_v, xr_v, pr_v, p0s_v, p0r_v, he_v, hr_v, edge_v, h0s_v, h0r_v,
    il_v, ic_v, fold_v, frecv_v, invs_v, base_v, sb_v, wn_v, wnr_v, co_v, g_v, tmp_v, do_v, sum_v, weight_s, node_s,
    load_sem, xsend, xrecv, psend, precv, p0send, p0recv, hsend, hrecv, h0send, h0recv,
    csend, crecv, gsend, grecv, osend, orecv, oload,
):
    s_at, h_at, r_at = lax.axis_index("scen"), lax.axis_index("hour"), lax.axis_index("reg")
    core = lax.rem(r_at, 2)
    other = 1 - core
    r_core = r_at + 1 - 2 * core
    r_chip = lax.rem(r_at + 2, 4)
    y_at, z_at = lax.rem(h_at, 4), lax.div(h_at, 4)

    def hour_rel(d):
        return lax.rem(z_at + d // 4, 4) * 4 + lax.rem(y_at + d % 4, 4)

    order = hop_order()
    left, right = lax.rem(h_at + NH - 1, NH), lax.rem(h_at + 1, NH)
    peer_core = (s_at, h_at, r_core)
    peer_chip = (s_at, h_at, r_chip)
    peer_o0 = (1 - s_at, h_at, r_at)
    peer_o1 = (1 - s_at, h_at, r_core)

    greeted = [(s_at, hour_rel(d), r) for d in order for r in (r_at, r_core)]
    greeted += [peer_core, peer_chip, peer_o0, peer_o1]
    barrier = pltpu.get_barrier_semaphore()
    for peer in greeted:
        pl.semaphore_signal(barrier, inc=1, device_id=peer, device_id_type=MESH)

    own_pair = pl.ds(2 * core, 2)
    oth_pair = pl.ds(2 * other, 2)
    own_cols = pl.ds(pl.multiple_of(core * COLS_CORE, COLS_CORE), COLS_CORE)
    body_rows = pl.ds(PAD, HOURS_LOCAL)

    def load(n, src, dst):
        cp = pltpu.make_async_copy(src, dst, load_sem.at[n])
        cp.start()
        return cp

    c_cap = load(0, cap_h, capl_v)
    c_edge0 = load(1, disp_h.at[:, pl.ds(0, 8), :], edge_v.at[0])
    c_edge1 = load(2, disp_h.at[:, pl.ds(HOURS_LOCAL - 8, 8), :], edge_v.at[1])
    c_tile = load(3, tile_h.at[0], tile_v)
    c_mask = load(4, mask_h.at[0], mask_v)
    c_inv = load(5, inv_h, il_v.at[0])
    c_mult = load(6, mult_h, il_v.at[1])
    c_cons = load(7, cons_h, il_v.at[2])
    c_ic = load(8, icost_h, ic_v)
    c_weight = load(15, weight_h, weight_s)
    c_node = load(16, node_h, node_s)
    c_disp = load(9, disp_h.at[own_pair], prim_v.at[0, :, body_rows, own_cols])
    c_a = load(10, cap_h.at[own_pair], a_v.at[:, :, own_cols])
    c_cost = load(11, cost_h.at[own_pair], cost_v.at[:, :, own_cols])
    c_dual = load(12, dual_h.at[own_pair], pre_v)
    c_dem = load(13, dem_h.at[own_pair], dem_v)

    c_cap.wait()
    for pair in range(2):
        for s in range(2):
            for i in range(4):
                p0s_v[pair, s, i:i + 1, :] = jnp.sum(
                    capl_v[2 * pair + s, :, 128 * i:128 * (i + 1)], axis=0, keepdims=True
                )
    p0r_v[core, h_at] = p0s_v[core]

    c_edge0.wait()
    c_edge1.wait()
    for s in range(4):
        h0s_v[0, s] = edge_v[0, s, 0:1, :]
        h0s_v[1, s] = edge_v[1, s, 7:8, :]

    c_tile.wait()
    c_mask.wait()
    ml_v[...] = tile_v[...] * mask_v[...].astype(BF16)

    c_inv.wait()
    c_mult.wait()
    c_cons.wait()
    c_ic.wait()
    for pair in range(2):
        for s in range(2):
            at = 2 * pair + s
            for g in range(3):
                cap0 = il_v[0, g, at:at + 1, :]
                base = ic_v[g:g + 1, :] + il_v[1, g, at:at + 1, :] - PENALTY * il_v[2, g, at:at + 1, :]
                for i in range(4):
                    lanes = slice(128 * i, 128 * (i + 1))
                    fold_v[pair, 0, s, g, i:i + 1, :] = cap0[:, lanes]
                    fold_v[pair, 1, s, g, i:i + 1, :] = base[:, lanes]

    c_weight.wait()
    c_node.wait()
    for s in range(4):
        for g in range(3):
            wn_v[4 * s + g:4 * s + g + 1, :] = jnp.full((1, 128), node_s[g, s].astype(F32), F32)
        wn_v[4 * s + 3:4 * s + 4, :] = jnp.full((1, 128), weight_s[s], F32)

    pl.semaphore_wait(barrier, len(greeted))

    def send(src, dst, ssem, rsem, peer):
        cp = pltpu.make_async_remote_copy(
            src_ref=src, dst_ref=dst, send_sem=ssem, recv_sem=rsem, device_id=peer, device_id_type=MESH
        )
        cp.start()
        return cp

    def swap(n, s):
        return [
            send(disp_h.at[2 * other + s], prim_v.at[0, s, body_rows, own_cols], csend.at[n], crecv.at[n], peer_core),
            send(cap_h.at[2 * other + s], a_v.at[s, :, own_cols], csend.at[n + 1], crecv.at[n + 1], peer_core),
            send(cost_h.at[2 * other + s], cost_v.at[s, :, own_cols], csend.at[n + 2], crecv.at[n + 2], peer_core),
        ]

    start_halo = []
    for side, to in ((0, left), (1, right)):
        for cross in (0, 1):
            peer = (s_at, to, r_core if cross else r_at)
            pair = oth_pair if cross else own_pair
            start_halo.append(send(
                h0s_v.at[side, pair], h0r_v.at[1 - side, core],
                h0send.at[side, cross], h0recv.at[side, cross], peer,
            ))
    first = []
    for d in order + [0]:
        for cross in (0, 1):
            if d == 0 and cross == 0:
                continue
            peer = (s_at, hour_rel(d), r_core if cross else r_at)
            first.append(send(
                p0s_v.at[other if cross else core], p0r_v.at[core, h_at],
                p0send.at[cross, d], p0recv.at[cross, d], peer,
            ))
        if d == order[0]:
            swap_m = send(ml_v, m_v.at[:, own_cols], csend.at[0], crecv.at[0], peer_core)
            swap_s = [swap(2, 0)]
    swap_s.append(swap(5, 1))
    swap_f = send(fold_v.at[other], frecv_v, csend.at[1], crecv.at[1], peer_core)
    weights = send(wn_v, wnr_v, csend.at[8], crecv.at[8], peer_o0)
    c_ml = load(14, ml_v, m_v.at[:, own_cols])

    sb_v[...] = jnp.zeros_like(sb_v)
    c_ml.wait()
    swap_m.wait()
    for j in range(4):
        mt_v[256 * j:256 * (j + 1), :] = m_v[:, 256 * j:256 * (j + 1)].T
    keep_left = jnp.where(h_at > 0, 1.0, 0.0).astype(F32)
    keep_right = jnp.where(h_at < NH - 1, 1.0, 0.0).astype(F32)
    c_disp.wait()
    c_a.wait()
    c_cost.wait()
    c_dual.wait()
    c_dem.wait()

    def prepare():
        swap_f.wait()
        for s in range(2):
            for g in range(3):
                for n, dest in ((0, invs_v), (1, base_v)):
                    mine, its = fold_v[core, n, s, g], frecv_v[n, s, g]
                    dest[s, g] = jnp.concatenate(
                        [jnp.where(core == 0, mine, its), jnp.where(core == 0, its, mine)], axis=0
                    )

    def coefficients():
        weights.wait()

        def row_of(s, g):
            ref = wn_v if s < 4 else wnr_v
            at = 4 * (s % 4) + g
            return ref[at:at + 1, :]

        for g in range(3):
            nodes = [row_of(s, g) for s in range(8)]
            for s in range(4):
                parts = [jnp.where(nodes[t] == nodes[s], row_of(t, 3), 0.0) for t in range(8)]
                mass = ((parts[0] + parts[1]) + (parts[2] + parts[3])) + ((parts[4] + parts[5]) + (parts[6] + parts[7]))
                scale = 1.0 / (mass + jnp.where(mass <= 0.0, 1.0, 0.0))
                for t in range(8):
                    at = (3 * s + g) * 8 + t
                    co_v[at:at + 1, :] = parts[t] * scale

    def image_copy(slot, s, half):
        rows = pl.ds(*SENT[half])
        return pltpu.make_async_remote_copy(
            src_ref=xs_v.at[s, rows], dst_ref=xr_v.at[slot, s, rows],
            send_sem=xsend.at[s, half], recv_sem=xrecv.at[slot, s, half],
            device_id=peer_chip, device_id_type=MESH,
        )

    def halo_copy(slot, side, s):
        return pltpu.make_async_remote_copy(
            src_ref=he_v.at[side, s], dst_ref=hr_v.at[slot, 1 - side, s],
            send_sem=hsend.at[side, s], recv_sem=hrecv.at[slot, 1 - side, s],
            device_id=(s_at, left if side == 0 else right, r_at), device_id_type=MESH,
        )

    def sum_copy(slot, d):
        return pltpu.make_async_remote_copy(
            src_ref=pr_v.at[slot, h_at], dst_ref=pr_v.at[slot, h_at],
            send_sem=psend.at[slot], recv_sem=precv.at[slot],
            device_id=(s_at, hour_rel(d), r_at), device_id_type=MESH,
        )

    def all_sums(slot, sem):
        block = pr_v.at[slot, pl.ds(0, NH - 1)]
        return pltpu.make_async_copy(block, block, sem.at[slot])

    def rows_of(ref, s, half, cols=slice(None)):
        parts = [ref[s, r0:r0 + n, cols] for r0, n in PARTS[half]]
        return parts[0] if len(parts) == 1 else jnp.concatenate(parts, axis=0)

    def put_rows(ref, s, half, value):
        at = 0
        for r0, n in PARTS[half]:
            ref[s, r0:r0 + n, :] = value[at:at + n]
            at += n

    def dual_update(last, s, half):
        image_copy(last, s, half).wait_recv()
        at, m = SENT[half]
        got = xr_v[last, s, at:at + m, :].astype(F32)
        got = jnp.concatenate([got[:m // 2], got[m // 2:]], axis=1)
        put_rows(pre_v, s, half, jnp.maximum(rows_of(pre_v, s, half) - STEP_DUAL * got, 0.0))

    def chunk(k, now, s, half):
        nxt = 1 - now

        @pl.when(k > 0)
        def _():
            dual_update(nxt, s, half)

        if half == 0:
            @pl.when(k > 0)
            def _():
                for side in range(2):
                    halo_copy(now, side, s).wait_recv()
                prim_v[now, s, PAD - 1:PAD, :] = hr_v[now, 0, s] * keep_left
                prim_v[now, s, PAD + HOURS_LOCAL:PAD + HOURS_LOCAL + 1, :] = hr_v[now, 1, s] * keep_right

            @pl.when(k == 0)
            def _():
                if s == 0:
                    for cp in start_halo:
                        cp.wait()
                for src in range(2):
                    lanes = slice(COLS_CORE * src, COLS_CORE * (src + 1))
                    prim_v[0, s, PAD - 1:PAD, lanes] = h0r_v[0, src, s] * keep_left
                    prim_v[0, s, PAD + HOURS_LOCAL:PAD + HOURS_LOCAL + 1, lanes] = h0r_v[1, src, s] * keep_right
        else:
            @pl.when(k == 0)
            def _():
                for cp in swap_s[s]:
                    cp.wait()

        dual = rows_of(pre_v, s, half)
        low = dual.astype(BF16)
        image = None
        for j in range(4):
            cols = slice(256 * j, 256 * (j + 1))
            pulled_all = jnp.dot(low, m_v[:, cols], preferred_element_type=F32)
            sb = jnp.concatenate([sb_v[s, 2 * j:2 * j + 1, :], sb_v[s, 2 * j + 1:2 * j + 2, :]], axis=1)
            exts = []
            at = 0
            for r0, n in PARTS[half]:
                pulled = pulled_all[at:at + n]
                at += n
                p = prim_v[now, s, PAD + r0:PAD + r0 + n, cols]
                up = prim_v[now, s, PAD + r0 - 1:PAD + r0 + n - 1, cols]
                down = prim_v[now, s, PAD + r0 + 1:PAD + r0 + n + 1, cols]
                cap = jnp.maximum(a_v[s, r0:r0 + n, cols] - sb, 0.0)
                rest = (cost_v[s, r0:r0 + n, cols] - pulled) + cap
                fresh = (
                    (1.0 - 2.0 * RAMP_WEIGHT * STEP_PRIMAL) * p
                    + (RAMP_WEIGHT * STEP_PRIMAL) * (up + down)
                    - STEP_PRIMAL * rest
                )
                fresh = jnp.maximum(fresh, 0.0)
                ext = 2.0 * fresh - p
                prim_v[nxt, s, PAD + r0:PAD + r0 + n, cols] = fresh
                a_v[s, r0:r0 + n, cols] = cap + STEP_CAP * ext
                exts.append(ext)
            ext_all = exts[0] if len(exts) == 1 else jnp.concatenate(exts, axis=0)
            part = jnp.dot(ext_all.astype(BF16), mt_v[cols, :], preferred_element_type=F32)
            image = part if image is None else image + part

        if half == 0:
            @pl.when(k < ITERS - 1)
            def _():
                for side, row in ((0, PAD), (1, PAD + HOURS_LOCAL - 1)):
                    @pl.when(k > 0)
                    def _():
                        halo_copy(nxt, side, s).wait_send()

                    he_v[side, s] = prim_v[nxt, s, row:row + 1, :]
                    halo_copy(nxt, side, s).start()

        @pl.when(k > 0)
        def _():
            image_copy(now, s, half).wait_send()

        at, m = SENT[half]
        xs_v[s, at:at + m, :] = jnp.concatenate([image[:, :128], image[:, 128:]], axis=0).astype(BF16)
        image_copy(now, s, half).start()
        put_rows(pre_v, s, half, dual + STEP_DUAL * (rows_of(dem_v, s, half) - image))

    def invest_step(total, s):
        mean = total * (1.0 / (NH * HOURS_LOCAL))
        spent = None
        for g in range(3):
            inv = invs_v[s, g]
            grad = base_v[s, g] + PENALTY * inv - mean
            new = jnp.maximum(inv - STEP_INVEST * grad, 0.0)
            invs_v[s, g] = new
            ext = 2.0 * new - inv
            spent = ext if spent is None else spent + ext
        sb_v[s] = STEP_CAP * spent

    def sums_in(k, now):
        @pl.when(k == 0)
        def _():
            prepare()
            for cp in first:
                cp.wait()
            for s in range(2):
                parts = []
                for src in range(2):
                    total = p0r_v[src, 0, s]
                    for h in range(1, NH):
                        total = total + p0r_v[src, h, s]
                    parts.append(total)
                invest_step(jnp.concatenate(parts, axis=0), s)

        @pl.when(k > 0)
        def _():
            all_sums(now, precv).wait()
            parts = [pr_v[now, h].astype(F32) for h in range(NH)]
            while len(parts) > 1:
                parts = [parts[i] + parts[i + 1] for i in range(0, len(parts), 2)]
            for s in range(2):
                invest_step(parts[0][8 * s:8 * (s + 1)], s)

    def step(k, carry):
        now = lax.rem(k, 2)
        nxt = 1 - now
        for s in range(2):
            for half in (1, 0):
                chunk(k, now, s, half)
        sums_in(k, now)

        @pl.when(k < ITERS - 1)
        def _():
            for s in range(2):
                for j in range(8):
                    left_over = jnp.maximum(a_v[s, :, 128 * j:128 * (j + 1)] - sb_v[s, j:j + 1, :], 0.0)
                    at = 8 * s + j
                    sum_v[at:at + 1, :] = jnp.sum(left_over, axis=0, keepdims=True)
            pr_v[nxt, h_at] = sum_v[...].astype(BF16)
            for d in order:
                sum_copy(nxt, d).start()

        @pl.when(k > 0)
        def _():
            all_sums(now, psend).wait()

        @pl.when(k == 0)
        def _():
            coefficients()

        @pl.when(k == ITERS - 1)
        def _():
            g_v[0, core] = invs_v[...]

        return carry

    lax.fori_loop(0, ITERS, step, 0)

    gathers = [
        send(g_v.at[0, core], g_v.at[1, core], gsend.at[1], grecv.at[1], peer_o0),
        send(g_v.at[0, core], g_v.at[1, core], gsend.at[2], grecv.at[2], peer_o1),
        send(g_v.at[0, core], g_v.at[0, core], gsend.at[0], grecv.at[0], peer_core),
    ]
    end = ITERS % 2
    outs = [
        send(
            prim_v.at[end, :, body_rows, pl.ds(pl.multiple_of(other * COLS_CORE, COLS_CORE), COLS_CORE)],
            disp_o.at[own_pair], osend.at[0], orecv.at[0], peer_core,
        )
    ]
    c_own = pltpu.make_async_copy(prim_v.at[end, :, body_rows, own_cols], disp_o.at[own_pair], oload.at[0])
    c_own.start()

    on_first = jnp.where(r_at < 2, 1.0, 0.0).astype(F32) > 0.5
    for s in range(2):
        for half in range(2):
            image_copy(1 - end, s, half).wait_send()
            dual_update(1 - end, s, half)
        d = pre_v[s]
        d = jnp.where(on_first, d[:, :128], d[:, 128:]).T
        lo, hi = d[:64], d[64:]
        do_v[0, s] = jnp.where(core == 0, lo, hi)
        do_v[1, s] = jnp.where(core == 0, hi, lo)
    outs.append(send(do_v.at[1], dual_o.at[own_pair], osend.at[1], orecv.at[1], peer_core))
    c_dual_own = pltpu.make_async_copy(do_v.at[0], dual_o.at[own_pair], oload.at[1])
    c_dual_own.start()
    for side in range(2):
        for s in range(2):
            halo_copy(end, side, s).wait_send()

    for cp in gathers[::-1]:
        cp.wait()
    for g in range(3):
        invs = [g_v[t // 4, (t // 2) % 2, t % 2, g] for t in range(8)]
        for s in range(4):
            spread = None
            for t in range(8):
                at = (3 * s + g) * 8 + t
                term = co_v[at:at + 1, :] * invs[t]
                spread = term if spread is None else spread + term
            tmp_v[0, 3 * s + g] = invs[s]
            tmp_v[1, 3 * s + g] = PENALTY * (invs[s] - spread)
    for s in range(4):
        for g in range(3):
            for i in range(4):
                lanes = slice(128 * i, 128 * (i + 1))
                inv_o[g, s:s + 1, lanes] = tmp_v[0, 3 * s + g, pl.ds(4 * core + i, 1), :]
                mult_o[g, s:s + 1, lanes] = il_v[1, g, s:s + 1, lanes] + tmp_v[1, 3 * s + g, pl.ds(4 * core + i, 1), :]
    for cp in outs:
        cp.wait()
    c_own.wait()
    c_dual_own.wait()


def hand_over(disp_i, dual_i, inv_i, mult_i, disp_o, dual_o, inv_o, mult_o, sem):
    copies = []
    pairs = [(inv_i, inv_o), (mult_i, mult_o)]
    for s in range(4):
        pairs.append((disp_i.at[s], disp_o.at[s]))
    pairs.append((dual_i, dual_o))
    for n, (src, dst) in enumerate(pairs):
        copies.append(pltpu.make_async_copy(src, dst, sem.at[n]))
    for cp in copies:
        cp.start()
    for cp in copies:
        cp.wait()


def shards(*args):
    args = args[:8] + tuple(jnp.transpose(x, (1, 0, 2)) for x in args[8:11]) + args[11:]
    hbm = pl.BlockSpec(memory_space=pltpu.HBM)
    vmem = pl.BlockSpec(memory_space=pltpu.VMEM)
    dma = pltpu.SemaphoreType.DMA
    disp, dual, inv, mult = pl.pallas_call(
        kernel,
        out_shape=(
            pltpu.VMEM((4, HOURS_LOCAL, COLS_CORE), F32),
            pltpu.VMEM((4, 64, HOURS_LOCAL), F32),
            pltpu.VMEM((3, 4, COLS_CORE), F32),
            pltpu.VMEM((3, 4, COLS_CORE), F32),
        ),
        in_specs=[hbm] * 13,
        out_specs=(vmem,) * 4,
        scratch_shapes=[
            pltpu.VMEM((2, HOURS_LOCAL, COLS), F32),
            pltpu.VMEM((2, 2, HOURS_LOCAL + 2 * PAD, COLS), F32),
            pltpu.VMEM((2, HOURS_LOCAL, COLS), F32),
            pltpu.VMEM((4, HOURS_LOCAL, COLS_CORE), F32),
            pltpu.VMEM((CONS, COLS_CORE), BF16),
            pltpu.VMEM((CONS, COLS_CORE), jnp.int32),
            pltpu.VMEM((CONS, COLS_CORE), BF16),
            pltpu.VMEM((CONS, COLS), BF16),
            pltpu.VMEM((COLS, CONS), BF16),
            pltpu.VMEM((2, HOURS_LOCAL, CONS), F32),
            pltpu.VMEM((2, HOURS_LOCAL, CONS), F32),
            pltpu.VMEM((2, 2 * HOURS_LOCAL, 128), BF16),
            pltpu.VMEM((2, 2, 2 * HOURS_LOCAL, 128), BF16),
            pltpu.VMEM((2, NH, 16, 128), BF16),
            pltpu.VMEM((2, 2, 4, 128), F32),
            pltpu.VMEM((2, NH, 2, 4, 128), F32),
            pltpu.VMEM((2, 2, 1, COLS), F32),
            pltpu.VMEM((2, 2, 2, 1, COLS), F32),
            pltpu.VMEM((2, 4, 8, COLS_CORE), F32),
            pltpu.VMEM((2, 4, 1, COLS_CORE), F32),
            pltpu.VMEM((2, 2, 2, 1, COLS_CORE), F32),
            pltpu.VMEM((3, 3, 4, COLS_CORE), F32),
            pltpu.VMEM((3, COLS_CORE), F32),
            pltpu.VMEM((2, 2, 2, 3, 4, 128), F32),
            pltpu.VMEM((2, 2, 3, 4, 128), F32),
            pltpu.VMEM((2, 3, 8, 128), F32),
            pltpu.VMEM((2, 3, 8, 128), F32),
            pltpu.VMEM((2, 8, 128), F32),
            pltpu.VMEM((16, 128), F32),
            pltpu.VMEM((16, 128), F32),
            pltpu.VMEM((96, 128), F32),
            pltpu.VMEM((2, 2, 2, 3, 8, 128), F32),
            pltpu.VMEM((2, 12, 8, 128), F32),
            pltpu.VMEM((2, 2, 64, HOURS_LOCAL), F32),
            pltpu.VMEM((16, 128), F32),
            pltpu.SMEM((4,), F32),
            pltpu.SMEM((3, 4), jnp.int32),
            dma((17,)),
            dma((2, 2)), dma((2, 2, 2)),
            dma((2,)), dma((2,)),
            dma((2, NH)), dma((2, NH)),
            dma((2, 2)), dma((2, 2, 2)),
            dma((2, 2)), dma((2, 2)),
            dma((9,)), dma((9,)),
            dma((3,)), dma((3,)),
            dma((2,)), dma((2,)), dma((2,)),
        ],
        compiler_params=pltpu.CompilerParams(
            collective_id=0, has_side_effects=True, vmem_limit_bytes=58 * 2**20
        ),
        cost_estimate=pl.CostEstimate(flops=3 * 10**9, bytes_accessed=9 * 10**6, transcendentals=0),
    )(*args)
    disp, dual, inv, mult = pl.pallas_call(
        hand_over,
        out_shape=tuple(jax.ShapeDtypeStruct(x.shape, x.dtype) for x in (disp, dual, inv, mult)),
        in_specs=[vmem] * 4,
        out_specs=(hbm,) * 4,
        scratch_shapes=[dma((7,))],
        compiler_params=pltpu.CompilerParams(vmem_limit_bytes=2**20),
        cost_estimate=pl.CostEstimate(flops=0, bytes_accessed=3 * 10**6, transcendentals=0),
    )(disp, dual, inv, mult)
    return disp, jnp.transpose(dual, (0, 2, 1)), jnp.transpose(inv, (1, 0, 2)), jnp.transpose(mult, (1, 0, 2))


def solution(mesh):
    placed = (
        P("scen", "hour", "reg"),
        P(None, "reg"),
        P("hour", None, "reg"),
        P("hour", None, "reg"),
        P("scen", "hour", None),
        P("scen", "hour", "reg"),
        P("scen", "hour", None),
        P("scen", "hour", "reg"),
        P("scen", None, "reg"),
        P("scen", None, "reg"),
        P("scen", None, "reg"),
        P("scen"),
        P(None, "scen"),
    )
    return jax.shard_map(
        shards,
        mesh=mesh,
        in_specs=placed,
        out_specs=(
            P("scen", "hour", "reg"),
            P("scen", "hour", "reg"),
            P("scen", None, "reg"),
            P("scen", None, "reg"),
        ),
        check_vma=False,
    )
```

```python
import jax
import jax.numpy as jnp
from jax import lax
from jax.experimental import pallas as pl
from jax.experimental.pallas import tpu as pltpu
from jax.sharding import PartitionSpec as P

ITERS = 8
RAMP_WEIGHT = 0.5
PENALTY = 1.0
STEP_PRIMAL = 0.3
STEP_INVEST = 0.5
STEP_DUAL = 0.3
STEP_CAP = 0.05

MESH = pl.DeviceIdType.MESH
HOURS_LOCAL = 168
PARTS = (((0, 40), (128, 40)), ((40, 88),))
SENT = ((0, 160), (160, 176))
NH = 16
COLS_CORE = 512
COLS = 1024
CONS = 256
PAD = 8
F32 = jnp.float32
BF16 = jnp.bfloat16


def hop_order():
    def hops(d):
        y, z = d % 4, d // 4
        return min(y, 4 - y) + min(z, 4 - z)

    return sorted(range(1, NH), key=lambda d: -hops(d))


def kernel(
    cost_h, icost_h, tile_h, mask_h, dem_h, disp_h, dual_h, cap_h, inv_h, mult_h, cons_h, weight_h, node_h,
    disp_o, dual_o, inv_o, mult_o,
    cost_v, prim_v, a_v, capl_v, tile_v, mask_v, ml_v, m_v, mt_v, pre_v, dem_v,
    xs_v, xr_v, pr_v, p0s_v, p0r_v, he_v, hr_v, edge_v, h0s_v, h0r_v,
    il_v, ic_v, fold_v, frecv_v, invs_v, base_v, sb_v, wn_v, wnr_v, co_v, g_v, tmp_v, do_v, sum_v, weight_s, node_s,
    load_sem, xsend, xrecv, psend, precv, p0send, p0recv, hsend, hrecv, h0send, h0recv,
    csend, crecv, gsend, grecv, osend, orecv, oload,
):
    s_at, h_at, r_at = lax.axis_index("scen"), lax.axis_index("hour"), lax.axis_index("reg")
    core = lax.rem(r_at, 2)
    other = 1 - core
    r_core = r_at + 1 - 2 * core
    r_chip = lax.rem(r_at + 2, 4)
    y_at, z_at = lax.rem(h_at, 4), lax.div(h_at, 4)

    def hour_rel(d):
        return lax.rem(z_at + d // 4, 4) * 4 + lax.rem(y_at + d % 4, 4)

    order = hop_order()
    left, right = lax.rem(h_at + NH - 1, NH), lax.rem(h_at + 1, NH)
    peer_core = (s_at, h_at, r_core)
    peer_chip = (s_at, h_at, r_chip)
    peer_o0 = (1 - s_at, h_at, r_at)
    peer_o1 = (1 - s_at, h_at, r_core)

    greeted = [(s_at, hour_rel(d), r) for d in order for r in (r_at, r_core)]
    greeted += [peer_core, peer_chip, peer_o0, peer_o1]
    barrier = pltpu.get_barrier_semaphore()
    for peer in greeted:
        pl.semaphore_signal(barrier, inc=1, device_id=peer, device_id_type=MESH)

    own_pair = pl.ds(2 * core, 2)
    oth_pair = pl.ds(2 * other, 2)
    own_cols = pl.ds(pl.multiple_of(core * COLS_CORE, COLS_CORE), COLS_CORE)
    body_rows = pl.ds(PAD, HOURS_LOCAL)

    def load(n, src, dst):
        cp = pltpu.make_async_copy(src, dst, load_sem.at[n])
        cp.start()
        return cp

    c_cap = load(0, cap_h, capl_v)
    c_edge0 = load(1, disp_h.at[:, pl.ds(0, 8), :], edge_v.at[0])
    c_edge1 = load(2, disp_h.at[:, pl.ds(HOURS_LOCAL - 8, 8), :], edge_v.at[1])
    c_tile = load(3, tile_h.at[0], tile_v)
    c_mask = load(4, mask_h.at[0], mask_v)
    c_inv = load(5, inv_h, il_v.at[0])
    c_mult = load(6, mult_h, il_v.at[1])
    c_cons = load(7, cons_h, il_v.at[2])
    c_ic = load(8, icost_h, ic_v)
    c_weight = load(15, weight_h, weight_s)
    c_node = load(16, node_h, node_s)
    c_disp = load(9, disp_h.at[own_pair], prim_v.at[0, :, body_rows, own_cols])
    c_a = load(10, cap_h.at[own_pair], a_v.at[:, :, own_cols])
    c_cost = load(11, cost_h.at[own_pair], cost_v.at[:, :, own_cols])
    c_dual = load(12, dual_h.at[own_pair], pre_v)
    c_dem = load(13, dem_h.at[own_pair], dem_v)

    c_cap.wait()
    for pair in range(2):
        for s in range(2):
            for i in range(4):
                p0s_v[pair, s, i:i + 1, :] = jnp.sum(
                    capl_v[2 * pair + s, :, 128 * i:128 * (i + 1)], axis=0, keepdims=True
                )
    p0r_v[core, h_at] = p0s_v[core]

    c_edge0.wait()
    c_edge1.wait()
    for s in range(4):
        h0s_v[0, s] = edge_v[0, s, 0:1, :]
        h0s_v[1, s] = edge_v[1, s, 7:8, :]

    c_tile.wait()
    c_mask.wait()
    ml_v[...] = tile_v[...] * mask_v[...].astype(BF16)

    c_inv.wait()
    c_mult.wait()
    c_cons.wait()
    c_ic.wait()
    for pair in range(2):
        for s in range(2):
            at = 2 * pair + s
            for g in range(3):
                cap0 = il_v[0, g, at:at + 1, :]
                base = ic_v[g:g + 1, :] + il_v[1, g, at:at + 1, :] - PENALTY * il_v[2, g, at:at + 1, :]
                for i in range(4):
                    lanes = slice(128 * i, 128 * (i + 1))
                    fold_v[pair, 0, s, g, i:i + 1, :] = cap0[:, lanes]
                    fold_v[pair, 1, s, g, i:i + 1, :] = base[:, lanes]

    c_weight.wait()
    c_node.wait()
    for s in range(4):
        for g in range(3):
            wn_v[4 * s + g:4 * s + g + 1, :] = jnp.full((1, 128), node_s[g, s].astype(F32), F32)
        wn_v[4 * s + 3:4 * s + 4, :] = jnp.full((1, 128), weight_s[s], F32)

    pl.semaphore_wait(barrier, len(greeted))

    def send(src, dst, ssem, rsem, peer):
        cp = pltpu.make_async_remote_copy(
            src_ref=src, dst_ref=dst, send_sem=ssem, recv_sem=rsem, device_id=peer, device_id_type=MESH
        )
        cp.start()
        return cp

    def swap(n, s):
        return [
            send(disp_h.at[2 * other + s], prim_v.at[0, s, body_rows, own_cols], csend.at[n], crecv.at[n], peer_core),
            send(cap_h.at[2 * other + s], a_v.at[s, :, own_cols], csend.at[n + 1], crecv.at[n + 1], peer_core),
            send(cost_h.at[2 * other + s], cost_v.at[s, :, own_cols], csend.at[n + 2], crecv.at[n + 2], peer_core),
        ]

    swap_m = send(ml_v, m_v.at[:, own_cols], csend.at[0], crecv.at[0], peer_core)
    swap_s = [swap(2, 0), swap(5, 1)]
    start_halo = []
    for side, to in ((0, left), (1, right)):
        for cross in (0, 1):
            peer = (s_at, to, r_core if cross else r_at)
            pair = oth_pair if cross else own_pair
            start_halo.append(send(
                h0s_v.at[side, pair], h0r_v.at[1 - side, core],
                h0send.at[side, cross], h0recv.at[side, cross], peer,
            ))
    first = []
    for d in order + [0]:
        for cross in (0, 1):
            if d == 0 and cross == 0:
                continue
            peer = (s_at, hour_rel(d), r_core if cross else r_at)
            first.append(send(
                p0s_v.at[other if cross else core], p0r_v.at[core, h_at],
                p0send.at[cross, d], p0recv.at[cross, d], peer,
            ))
    swap_f = send(fold_v.at[other], frecv_v, csend.at[1], crecv.at[1], peer_core)
    weights = send(wn_v, wnr_v, csend.at[8], crecv.at[8], peer_o0)
    c_ml = load(14, ml_v, m_v.at[:, own_cols])

    sb_v[...] = jnp.zeros_like(sb_v)
    c_ml.wait()
    swap_m.wait()
    for j in range(4):
        mt_v[256 * j:256 * (j + 1), :] = m_v[:, 256 * j:256 * (j + 1)].T
    keep_left = jnp.where(h_at > 0, 1.0, 0.0).astype(F32)
    keep_right = jnp.where(h_at < NH - 1, 1.0, 0.0).astype(F32)
    c_disp.wait()
    c_a.wait()
    c_cost.wait()
    c_dual.wait()
    c_dem.wait()

    def prepare():
        swap_f.wait()
        for s in range(2):
            for g in range(3):
                for n, dest in ((0, invs_v), (1, base_v)):
                    mine, its = fold_v[core, n, s, g], frecv_v[n, s, g]
                    dest[s, g] = jnp.concatenate(
                        [jnp.where(core == 0, mine, its), jnp.where(core == 0, its, mine)], axis=0
                    )

    def coefficients():
        weights.wait()

        def row_of(s, g):
            ref = wn_v if s < 4 else wnr_v
            at = 4 * (s % 4) + g
            return ref[at:at + 1, :]

        for g in range(3):
            nodes = [row_of(s, g) for s in range(8)]
            for s in range(4):
                parts = [jnp.where(nodes[t] == nodes[s], row_of(t, 3), 0.0) for t in range(8)]
                mass = ((parts[0] + parts[1]) + (parts[2] + parts[3])) + ((parts[4] + parts[5]) + (parts[6] + parts[7]))
                scale = 1.0 / (mass + jnp.where(mass <= 0.0, 1.0, 0.0))
                for t in range(8):
                    at = (3 * s + g) * 8 + t
                    co_v[at:at + 1, :] = parts[t] * scale

    def image_copy(slot, s, half):
        rows = pl.ds(*SENT[half])
        return pltpu.make_async_remote_copy(
            src_ref=xs_v.at[s, rows], dst_ref=xr_v.at[slot, s, rows],
            send_sem=xsend.at[s, half], recv_sem=xrecv.at[slot, s, half],
            device_id=peer_chip, device_id_type=MESH,
        )

    def halo_copy(slot, side, s):
        return pltpu.make_async_remote_copy(
            src_ref=he_v.at[side, s], dst_ref=hr_v.at[slot, 1 - side, s],
            send_sem=hsend.at[side, s], recv_sem=hrecv.at[slot, 1 - side, s],
            device_id=(s_at, left if side == 0 else right, r_at), device_id_type=MESH,
        )

    def sum_copy(slot, d):
        return pltpu.make_async_remote_copy(
            src_ref=pr_v.at[slot, h_at], dst_ref=pr_v.at[slot, h_at],
            send_sem=psend.at[slot], recv_sem=precv.at[slot],
            device_id=(s_at, hour_rel(d), r_at), device_id_type=MESH,
        )

    def all_sums(slot, sem):
        block = pr_v.at[slot, pl.ds(0, NH - 1)]
        return pltpu.make_async_copy(block, block, sem.at[slot])

    def rows_of(ref, s, half, cols=slice(None)):
        parts = [ref[s, r0:r0 + n, cols] for r0, n in PARTS[half]]
        return parts[0] if len(parts) == 1 else jnp.concatenate(parts, axis=0)

    def put_rows(ref, s, half, value):
        at = 0
        for r0, n in PARTS[half]:
            ref[s, r0:r0 + n, :] = value[at:at + n]
            at += n

    def dual_update(last, s, half):
        image_copy(last, s, half).wait_recv()
        at, m = SENT[half]
        got = xr_v[last, s, at:at + m, :].astype(F32)
        got = jnp.concatenate([got[:m // 2], got[m // 2:]], axis=1)
        put_rows(pre_v, s, half, jnp.maximum(rows_of(pre_v, s, half) - STEP_DUAL * got, 0.0))

    def chunk(k, now, s, half):
        nxt = 1 - now

        @pl.when(k > 0)
        def _():
            dual_update(nxt, s, half)

        if half == 0:
            @pl.when(k > 0)
            def _():
                for side in range(2):
                    halo_copy(now, side, s).wait_recv()
                prim_v[now, s, PAD - 1:PAD, :] = hr_v[now, 0, s] * keep_left
                prim_v[now, s, PAD + HOURS_LOCAL:PAD + HOURS_LOCAL + 1, :] = hr_v[now, 1, s] * keep_right

            @pl.when(k == 0)
            def _():
                if s == 0:
                    for cp in start_halo:
                        cp.wait()
                for src in range(2):
                    lanes = slice(COLS_CORE * src, COLS_CORE * (src + 1))
                    prim_v[0, s, PAD - 1:PAD, lanes] = h0r_v[0, src, s] * keep_left
                    prim_v[0, s, PAD + HOURS_LOCAL:PAD + HOURS_LOCAL + 1, lanes] = h0r_v[1, src, s] * keep_right
        else:
            @pl.when(k == 0)
            def _():
                for cp in swap_s[s]:
                    cp.wait()

        dual = rows_of(pre_v, s, half)
        low = dual.astype(BF16)
        image = None
        for j in range(4):
            cols = slice(256 * j, 256 * (j + 1))
            pulled_all = jnp.dot(low, m_v[:, cols], preferred_element_type=F32)
            sb = jnp.concatenate([sb_v[s, 2 * j:2 * j + 1, :], sb_v[s, 2 * j + 1:2 * j + 2, :]], axis=1)
            exts = []
            at = 0
            for r0, n in PARTS[half]:
                pulled = pulled_all[at:at + n]
                at += n
                p = prim_v[now, s, PAD + r0:PAD + r0 + n, cols]
                up = prim_v[now, s, PAD + r0 - 1:PAD + r0 + n - 1, cols]
                down = prim_v[now, s, PAD + r0 + 1:PAD + r0 + n + 1, cols]
                cap = jnp.maximum(a_v[s, r0:r0 + n, cols] - sb, 0.0)
                rest = (cost_v[s, r0:r0 + n, cols] - pulled) + cap
                fresh = (
                    (1.0 - 2.0 * RAMP_WEIGHT * STEP_PRIMAL) * p
                    + (RAMP_WEIGHT * STEP_PRIMAL) * (up + down)
                    - STEP_PRIMAL * rest
                )
                fresh = jnp.maximum(fresh, 0.0)
                ext = 2.0 * fresh - p
                prim_v[nxt, s, PAD + r0:PAD + r0 + n, cols] = fresh
                a_v[s, r0:r0 + n, cols] = cap + STEP_CAP * ext
                exts.append(ext)
            ext_all = exts[0] if len(exts) == 1 else jnp.concatenate(exts, axis=0)
            part = jnp.dot(ext_all.astype(BF16), mt_v[cols, :], preferred_element_type=F32)
            image = part if image is None else image + part

        if half == 0:
            @pl.when(k < ITERS - 1)
            def _():
                for side, row in ((0, PAD), (1, PAD + HOURS_LOCAL - 1)):
                    @pl.when(k > 0)
                    def _():
                        halo_copy(nxt, side, s).wait_send()

                    he_v[side, s] = prim_v[nxt, s, row:row + 1, :]
                    halo_copy(nxt, side, s).start()

        @pl.when(k > 0)
        def _():
            image_copy(now, s, half).wait_send()

        at, m = SENT[half]
        xs_v[s, at:at + m, :] = jnp.concatenate([image[:, :128], image[:, 128:]], axis=0).astype(BF16)
        image_copy(now, s, half).start()
        put_rows(pre_v, s, half, dual + STEP_DUAL * (rows_of(dem_v, s, half) - image))

    def invest_step(total, s):
        mean = total * (1.0 / (NH * HOURS_LOCAL))
        spent = None
        for g in range(3):
            inv = invs_v[s, g]
            grad = base_v[s, g] + PENALTY * inv - mean
            new = jnp.maximum(inv - STEP_INVEST * grad, 0.0)
            invs_v[s, g] = new
            ext = 2.0 * new - inv
            spent = ext if spent is None else spent + ext
        sb_v[s] = STEP_CAP * spent

    def first_sums():
        prepare()
        for cp in first:
            cp.wait()
        for s in range(2):
            parts = []
            for src in range(2):
                total = p0r_v[src, 0, s]
                for h in range(1, NH):
                    total = total + p0r_v[src, h, s]
                parts.append(total)
            invest_step(jnp.concatenate(parts, axis=0), s)

    def later_sums(now):
        all_sums(now, precv).wait()
        parts = [pr_v[now, h].astype(F32) for h in range(NH)]
        while len(parts) > 1:
            parts = [parts[i] + parts[i + 1] for i in range(0, len(parts), 2)]
        for s in range(2):
            invest_step(parts[0][8 * s:8 * (s + 1)], s)

    def sums_in(k, now):
        @pl.when(k == 0)
        def _():
            first_sums()

        @pl.when(k > 0)
        def _():
            later_sums(now)

    def step(k, carry):
        now = lax.rem(k, 2)
        nxt = 1 - now
        for half in (1, 0):
            for s in range(2):
                chunk(k, now, s, half)

        @pl.when(k < ITERS - 1)
        def _():
            sums_in(k, now)
            for s in range(2):
                for j in range(8):
                    left_over = jnp.maximum(a_v[s, :, 128 * j:128 * (j + 1)] - sb_v[s, j:j + 1, :], 0.0)
                    at = 8 * s + j
                    sum_v[at:at + 1, :] = jnp.sum(left_over, axis=0, keepdims=True)
            pr_v[nxt, h_at] = sum_v[...].astype(BF16)
            for d in order:
                sum_copy(nxt, d).start()

        @pl.when((k > 0) & (k < ITERS - 1))
        def _():
            all_sums(now, psend).wait()

        @pl.when(k == 0)
        def _():
            coefficients()

        return carry

    lax.fori_loop(0, ITERS, step, 0)

    end = ITERS % 2
    outs = [
        send(
            prim_v.at[end, :, body_rows, pl.ds(pl.multiple_of(other * COLS_CORE, COLS_CORE), COLS_CORE)],
            disp_o.at[own_pair], osend.at[0], orecv.at[0], peer_core,
        )
    ]
    c_own = pltpu.make_async_copy(prim_v.at[end, :, body_rows, own_cols], disp_o.at[own_pair], oload.at[0])
    c_own.start()

    later_sums(1 - end)
    g_v[0, core] = invs_v[...]
    gathers = [
        send(g_v.at[0, core], g_v.at[1, core], gsend.at[1], grecv.at[1], peer_o0),
        send(g_v.at[0, core], g_v.at[1, core], gsend.at[2], grecv.at[2], peer_o1),
        send(g_v.at[0, core], g_v.at[0, core], gsend.at[0], grecv.at[0], peer_core),
    ]
    all_sums(1 - end, psend).wait()

    on_first = jnp.where(r_at < 2, 1.0, 0.0).astype(F32) > 0.5
    for s in range(2):
        for half in range(2):
            image_copy(1 - end, s, half).wait_send()
            dual_update(1 - end, s, half)
        d = pre_v[s]
        d = jnp.where(on_first, d[:, :128], d[:, 128:]).T
        lo, hi = d[:64], d[64:]
        do_v[0, s] = jnp.where(core == 0, lo, hi)
        do_v[1, s] = jnp.where(core == 0, hi, lo)
    outs.append(send(do_v.at[1], dual_o.at[own_pair], osend.at[1], orecv.at[1], peer_core))
    c_dual_own = pltpu.make_async_copy(do_v.at[0], dual_o.at[own_pair], oload.at[1])
    c_dual_own.start()
    for side in range(2):
        for s in range(2):
            halo_copy(end, side, s).wait_send()

    def share(group, s, g):
        spread = None
        for t in range(4 * group, 4 * group + 4):
            at = (3 * s + g) * 8 + t
            term = co_v[at:at + 1, :] * g_v[group, (t // 2) % 2, t % 2, g]
            spread = term if spread is None else spread + term
        return spread

    gathers[2].wait()
    for g in range(3):
        for s in range(4):
            inv = g_v[0, s // 2, s % 2, g]
            tmp_v[0, 3 * s + g] = inv
            tmp_v[1, 3 * s + g] = inv - share(0, s, g)
    for s in range(4):
        for g in range(3):
            for i in range(4):
                lanes = slice(128 * i, 128 * (i + 1))
                inv_o[g, s:s + 1, lanes] = tmp_v[0, 3 * s + g, pl.ds(4 * core + i, 1), :]
    gathers[1].wait()
    gathers[0].wait()
    for g in range(3):
        for s in range(4):
            tmp_v[1, 3 * s + g] = PENALTY * (tmp_v[1, 3 * s + g] - share(1, s, g))
            for i in range(4):
                lanes = slice(128 * i, 128 * (i + 1))
                mult_o[g, s:s + 1, lanes] = il_v[1, g, s:s + 1, lanes] + tmp_v[1, 3 * s + g, pl.ds(4 * core + i, 1), :]
    for cp in outs:
        cp.wait()
    c_own.wait()
    c_dual_own.wait()


def hand_over(disp_i, dual_i, inv_i, mult_i, disp_o, dual_o, inv_o, mult_o, sem):
    copies = []
    pairs = [(inv_i, inv_o), (mult_i, mult_o)]
    for s in range(4):
        pairs.append((disp_i.at[s], disp_o.at[s]))
    pairs.append((dual_i, dual_o))
    for n, (src, dst) in enumerate(pairs):
        copies.append(pltpu.make_async_copy(src, dst, sem.at[n]))
    for cp in copies:
        cp.start()
    for cp in copies:
        cp.wait()


def shards(*args):
    args = args[:8] + tuple(jnp.transpose(x, (1, 0, 2)) for x in args[8:11]) + args[11:]
    hbm = pl.BlockSpec(memory_space=pltpu.HBM)
    vmem = pl.BlockSpec(memory_space=pltpu.VMEM)
    dma = pltpu.SemaphoreType.DMA
    disp, dual, inv, mult = pl.pallas_call(
        kernel,
        out_shape=(
            pltpu.VMEM((4, HOURS_LOCAL, COLS_CORE), F32),
            pltpu.VMEM((4, 64, HOURS_LOCAL), F32),
            pltpu.VMEM((3, 4, COLS_CORE), F32),
            pltpu.VMEM((3, 4, COLS_CORE), F32),
        ),
        in_specs=[hbm] * 13,
        out_specs=(vmem,) * 4,
        scratch_shapes=[
            pltpu.VMEM((2, HOURS_LOCAL, COLS), F32),
            pltpu.VMEM((2, 2, HOURS_LOCAL + 2 * PAD, COLS), F32),
            pltpu.VMEM((2, HOURS_LOCAL, COLS), F32),
            pltpu.VMEM((4, HOURS_LOCAL, COLS_CORE), F32),
            pltpu.VMEM((CONS, COLS_CORE), BF16),
            pltpu.VMEM((CONS, COLS_CORE), jnp.int32),
            pltpu.VMEM((CONS, COLS_CORE), BF16),
            pltpu.VMEM((CONS, COLS), BF16),
            pltpu.VMEM((COLS, CONS), BF16),
            pltpu.VMEM((2, HOURS_LOCAL, CONS), F32),
            pltpu.VMEM((2, HOURS_LOCAL, CONS), F32),
            pltpu.VMEM((2, 2 * HOURS_LOCAL, 128), BF16),
            pltpu.VMEM((2, 2, 2 * HOURS_LOCAL, 128), BF16),
            pltpu.VMEM((2, NH, 16, 128), BF16),
            pltpu.VMEM((2, 2, 4, 128), F32),
            pltpu.VMEM((2, NH, 2, 4, 128), F32),
            pltpu.VMEM((2, 2, 1, COLS), F32),
            pltpu.VMEM((2, 2, 2, 1, COLS), F32),
            pltpu.VMEM((2, 4, 8, COLS_CORE), F32),
            pltpu.VMEM((2, 4, 1, COLS_CORE), F32),
            pltpu.VMEM((2, 2, 2, 1, COLS_CORE), F32),
            pltpu.VMEM((3, 3, 4, COLS_CORE), F32),
            pltpu.VMEM((3, COLS_CORE), F32),
            pltpu.VMEM((2, 2, 2, 3, 4, 128), F32),
            pltpu.VMEM((2, 2, 3, 4, 128), F32),
            pltpu.VMEM((2, 3, 8, 128), F32),
            pltpu.VMEM((2, 3, 8, 128), F32),
            pltpu.VMEM((2, 8, 128), F32),
            pltpu.VMEM((16, 128), F32),
            pltpu.VMEM((16, 128), F32),
            pltpu.VMEM((96, 128), F32),
            pltpu.VMEM((2, 2, 2, 3, 8, 128), F32),
            pltpu.VMEM((2, 12, 8, 128), F32),
            pltpu.VMEM((2, 2, 64, HOURS_LOCAL), F32),
            pltpu.VMEM((16, 128), F32),
            pltpu.SMEM((4,), F32),
            pltpu.SMEM((3, 4), jnp.int32),
            dma((17,)),
            dma((2, 2)), dma((2, 2, 2)),
            dma((2,)), dma((2,)),
            dma((2, NH)), dma((2, NH)),
            dma((2, 2)), dma((2, 2, 2)),
            dma((2, 2)), dma((2, 2)),
            dma((9,)), dma((9,)),
            dma((3,)), dma((3,)),
            dma((2,)), dma((2,)), dma((2,)),
        ],
        compiler_params=pltpu.CompilerParams(
            collective_id=0, has_side_effects=True, vmem_limit_bytes=58 * 2**20
        ),
        cost_estimate=pl.CostEstimate(flops=3 * 10**9, bytes_accessed=9 * 10**6, transcendentals=0),
    )(*args)
    disp, dual, inv, mult = pl.pallas_call(
        hand_over,
        out_shape=tuple(jax.ShapeDtypeStruct(x.shape, x.dtype) for x in (disp, dual, inv, mult)),
        in_specs=[vmem] * 4,
        out_specs=(hbm,) * 4,
        scratch_shapes=[dma((7,))],
        compiler_params=pltpu.CompilerParams(vmem_limit_bytes=2**20),
        cost_estimate=pl.CostEstimate(flops=0, bytes_accessed=3 * 10**6, transcendentals=0),
    )(disp, dual, inv, mult)
    return disp, jnp.transpose(dual, (0, 2, 1)), jnp.transpose(inv, (1, 0, 2)), jnp.transpose(mult, (1, 0, 2))


def solution(mesh):
    placed = (
        P("scen", "hour", "reg"),
        P(None, "reg"),
        P("hour", None, "reg"),
        P("hour", None, "reg"),
        P("scen", "hour", None),
        P("scen", "hour", "reg"),
        P("scen", "hour", None),
        P("scen", "hour", "reg"),
        P("scen", None, "reg"),
        P("scen", None, "reg"),
        P("scen", None, "reg"),
        P("scen"),
        P(None, "scen"),
    )
    return jax.shard_map(
        shards,
        mesh=mesh,
        in_specs=placed,
        out_specs=(
            P("scen", "hour", "reg"),
            P("scen", "hour", "reg"),
            P("scen", None, "reg"),
            P("scen", None, "reg"),
        ),
        check_vma=False,
    )
```

```python
import jax
import jax.numpy as jnp
from jax import lax
from jax.experimental import pallas as pl
from jax.experimental.pallas import tpu as pltpu
from jax.sharding import PartitionSpec as P

ITERS = 8
RAMP_WEIGHT = 0.5
PENALTY = 1.0
STEP_PRIMAL = 0.3
STEP_INVEST = 0.5
STEP_DUAL = 0.3
STEP_CAP = 0.05

MESH = pl.DeviceIdType.MESH
HOURS_LOCAL = 168
PARTS = (((0, 40), (128, 40)), ((40, 88),))
SENT = ((0, 160), (160, 176))
NH = 16
COLS_CORE = 512
COLS = 1024
CONS = 256
PAD = 8
F32 = jnp.float32
BF16 = jnp.bfloat16


def hop_order():
    def hops(d):
        y, z = d % 4, d // 4
        return min(y, 4 - y) + min(z, 4 - z)

    return sorted(range(1, NH), key=lambda d: -hops(d))


def kernel(
    cost_h, icost_h, tile_h, mask_h, dem_h, disp_h, dual_h, cap_h, inv_h, mult_h, cons_h, weight_h, node_h,
    disp_o, dual_o, inv_o, mult_o,
    cost_v, prim_v, a_v, capl_v, tile_v, mask_v, ml_v, m_v, mt_v, pre_v, dem_v,
    xs_v, xr_v, pr_v, p0s_v, p0r_v, he_v, hr_v, edge_v, h0s_v, h0r_v,
    il_v, ic_v, fold_v, frecv_v, invs_v, base_v, sb_v, wn_v, wnr_v, co_v, g_v, tmp_v, do_v, sum_v, weight_s, node_s,
    load_sem, xsend, xrecv, psend, precv, p0send, p0recv, hsend, hrecv, h0send, h0recv,
    csend, crecv, gsend, grecv, osend, orecv, oload,
):
    s_at, h_at, r_at = lax.axis_index("scen"), lax.axis_index("hour"), lax.axis_index("reg")
    core = lax.rem(r_at, 2)
    other = 1 - core
    r_core = r_at + 1 - 2 * core
    r_chip = lax.rem(r_at + 2, 4)
    y_at, z_at = lax.rem(h_at, 4), lax.div(h_at, 4)

    def hour_rel(d):
        return lax.rem(z_at + d // 4, 4) * 4 + lax.rem(y_at + d % 4, 4)

    order = hop_order()
    left, right = lax.rem(h_at + NH - 1, NH), lax.rem(h_at + 1, NH)
    peer_core = (s_at, h_at, r_core)
    peer_chip = (s_at, h_at, r_chip)
    peer_o0 = (1 - s_at, h_at, r_at)
    peer_o1 = (1 - s_at, h_at, r_core)

    greeted = [(s_at, hour_rel(d), r) for d in order for r in (r_at, r_core)]
    greeted += [peer_core, peer_chip, peer_o0, peer_o1]
    barrier = pltpu.get_barrier_semaphore()
    for peer in greeted:
        pl.semaphore_signal(barrier, inc=1, device_id=peer, device_id_type=MESH)

    own_pair = pl.ds(2 * core, 2)
    oth_pair = pl.ds(2 * other, 2)
    own_cols = pl.ds(pl.multiple_of(core * COLS_CORE, COLS_CORE), COLS_CORE)
    body_rows = pl.ds(PAD, HOURS_LOCAL)

    def load(n, src, dst):
        cp = pltpu.make_async_copy(src, dst, load_sem.at[n])
        cp.start()
        return cp

    c_cap = load(0, cap_h, capl_v)
    c_edge0 = load(1, disp_h.at[:, pl.ds(0, 8), :], edge_v.at[0])
    c_edge1 = load(2, disp_h.at[:, pl.ds(HOURS_LOCAL - 8, 8), :], edge_v.at[1])
    c_tile = load(3, tile_h.at[0], tile_v)
    c_mask = load(4, mask_h.at[0], mask_v)
    c_inv = load(5, inv_h, il_v.at[0])
    c_mult = load(6, mult_h, il_v.at[1])
    c_cons = load(7, cons_h, il_v.at[2])
    c_ic = load(8, icost_h, ic_v)
    c_weight = load(15, weight_h, weight_s)
    c_node = load(16, node_h, node_s)
    c_disp = load(9, disp_h.at[own_pair], prim_v.at[0, :, body_rows, own_cols])
    c_a = load(10, cap_h.at[own_pair], a_v.at[:, :, own_cols])
    c_cost = load(11, cost_h.at[own_pair], cost_v.at[:, :, own_cols])
    c_dual = load(12, dual_h.at[own_pair], pre_v)
    c_dem = load(13, dem_h.at[own_pair], dem_v)

    c_cap.wait()
    for pair in range(2):
        for s in range(2):
            for i in range(4):
                p0s_v[pair, s, i:i + 1, :] = jnp.sum(
                    capl_v[2 * pair + s, :, 128 * i:128 * (i + 1)], axis=0, keepdims=True
                )
    p0r_v[core, h_at] = p0s_v[core]

    c_edge0.wait()
    c_edge1.wait()
    for s in range(4):
        h0s_v[0, s] = edge_v[0, s, 0:1, :]
        h0s_v[1, s] = edge_v[1, s, 7:8, :]

    c_tile.wait()
    c_mask.wait()
    ml_v[...] = tile_v[...] * mask_v[...].astype(BF16)

    c_inv.wait()
    c_mult.wait()
    c_cons.wait()
    c_ic.wait()
    for pair in range(2):
        for s in range(2):
            at = 2 * pair + s
            for g in range(3):
                cap0 = il_v[0, g, at:at + 1, :]
                base = ic_v[g:g + 1, :] + il_v[1, g, at:at + 1, :] - PENALTY * il_v[2, g, at:at + 1, :]
                for i in range(4):
                    lanes = slice(128 * i, 128 * (i + 1))
                    fold_v[pair, 0, s, g, i:i + 1, :] = cap0[:, lanes]
                    fold_v[pair, 1, s, g, i:i + 1, :] = base[:, lanes]

    c_weight.wait()
    c_node.wait()
    for s in range(4):
        for g in range(3):
            wn_v[4 * s + g:4 * s + g + 1, :] = jnp.full((1, 128), node_s[g, s].astype(F32), F32)
        wn_v[4 * s + 3:4 * s + 4, :] = jnp.full((1, 128), weight_s[s], F32)

    pl.semaphore_wait(barrier, len(greeted))

    def send(src, dst, ssem, rsem, peer):
        cp = pltpu.make_async_remote_copy(
            src_ref=src, dst_ref=dst, send_sem=ssem, recv_sem=rsem, device_id=peer, device_id_type=MESH
        )
        cp.start()
        return cp

    def swap(n, s):
        return [
            send(disp_h.at[2 * other + s], prim_v.at[0, s, body_rows, own_cols], csend.at[n], crecv.at[n], peer_core),
            send(cap_h.at[2 * other + s], a_v.at[s, :, own_cols], csend.at[n + 1], crecv.at[n + 1], peer_core),
            send(cost_h.at[2 * other + s], cost_v.at[s, :, own_cols], csend.at[n + 2], crecv.at[n + 2], peer_core),
        ]

    swap_m = send(ml_v, m_v.at[:, own_cols], csend.at[0], crecv.at[0], peer_core)
    swap_f = send(fold_v.at[other], frecv_v, csend.at[1], crecv.at[1], peer_core)
    swap_s = [swap(2, 0), swap(5, 1)]
    start_halo = []
    for side, to in ((0, left), (1, right)):
        for cross in (0, 1):
            peer = (s_at, to, r_core if cross else r_at)
            pair = oth_pair if cross else own_pair
            start_halo.append(send(
                h0s_v.at[side, pair], h0r_v.at[1 - side, core],
                h0send.at[side, cross], h0recv.at[side, cross], peer,
            ))
    first = []
    for d in order + [0]:
        for cross in (0, 1):
            if d == 0 and cross == 0:
                continue
            peer = (s_at, hour_rel(d), r_core if cross else r_at)
            first.append(send(
                p0s_v.at[other if cross else core], p0r_v.at[core, h_at],
                p0send.at[cross, d], p0recv.at[cross, d], peer,
            ))
    weights = send(wn_v, wnr_v, csend.at[8], crecv.at[8], peer_o0)
    c_ml = load(14, ml_v, m_v.at[:, own_cols])

    sb_v[...] = jnp.zeros_like(sb_v)
    c_ml.wait()
    swap_m.wait()
    for j in range(4):
        mt_v[256 * j:256 * (j + 1), :] = m_v[:, 256 * j:256 * (j + 1)].T
    keep_left = jnp.where(h_at > 0, 1.0, 0.0).astype(F32)
    keep_right = jnp.where(h_at < NH - 1, 1.0, 0.0).astype(F32)
    c_disp.wait()
    c_a.wait()
    c_cost.wait()
    c_dual.wait()
    c_dem.wait()

    def prepare():
        swap_f.wait()
        for s in range(2):
            for g in range(3):
                for n, dest in ((0, invs_v), (1, base_v)):
                    mine, its = fold_v[core, n, s, g], frecv_v[n, s, g]
                    dest[s, g] = jnp.concatenate(
                        [jnp.where(core == 0, mine, its), jnp.where(core == 0, its, mine)], axis=0
                    )

    def coefficients():
        weights.wait()

        def row_of(s, g):
            ref = wn_v if s < 4 else wnr_v
            at = 4 * (s % 4) + g
            return ref[at:at + 1, :]

        for g in range(3):
            nodes = [row_of(s, g) for s in range(8)]
            for s in range(4):
                parts = [jnp.where(nodes[t] == nodes[s], row_of(t, 3), 0.0) for t in range(8)]
                mass = ((parts[0] + parts[1]) + (parts[2] + parts[3])) + ((parts[4] + parts[5]) + (parts[6] + parts[7]))
                scale = 1.0 / (mass + jnp.where(mass <= 0.0, 1.0, 0.0))
                for t in range(8):
                    at = (3 * s + g) * 8 + t
                    co_v[at:at + 1, :] = parts[t] * scale

    def image_copy(slot, s, half):
        rows = pl.ds(*SENT[half])
        return pltpu.make_async_remote_copy(
            src_ref=xs_v.at[s, rows], dst_ref=xr_v.at[slot, s, rows],
            send_sem=xsend.at[s, half], recv_sem=xrecv.at[slot, s, half],
            device_id=peer_chip, device_id_type=MESH,
        )

    def halo_copy(slot, side, s):
        return pltpu.make_async_remote_copy(
            src_ref=he_v.at[side, s], dst_ref=hr_v.at[slot, 1 - side, s],
            send_sem=hsend.at[side, s], recv_sem=hrecv.at[slot, 1 - side, s],
            device_id=(s_at, left if side == 0 else right, r_at), device_id_type=MESH,
        )

    def sum_copy(slot, d):
        return pltpu.make_async_remote_copy(
            src_ref=pr_v.at[slot, h_at], dst_ref=pr_v.at[slot, h_at],
            send_sem=psend.at[slot], recv_sem=precv.at[slot],
            device_id=(s_at, hour_rel(d), r_at), device_id_type=MESH,
        )

    def all_sums(slot, sem):
        block = pr_v.at[slot, pl.ds(0, NH - 1)]
        return pltpu.make_async_copy(block, block, sem.at[slot])

    def rows_of(ref, s, half, cols=slice(None)):
        parts = [ref[s, r0:r0 + n, cols] for r0, n in PARTS[half]]
        return parts[0] if len(parts) == 1 else jnp.concatenate(parts, axis=0)

    def put_rows(ref, s, half, value):
        at = 0
        for r0, n in PARTS[half]:
            ref[s, r0:r0 + n, :] = value[at:at + n]
            at += n

    def dual_update(last, s, half):
        image_copy(last, s, half).wait_recv()
        at, m = SENT[half]
        got = xr_v[last, s, at:at + m, :].astype(F32)
        got = jnp.concatenate([got[:m // 2], got[m // 2:]], axis=1)
        put_rows(pre_v, s, half, jnp.maximum(rows_of(pre_v, s, half) - STEP_DUAL * got, 0.0))

    def chunk(k, now, s, half):
        nxt = 1 - now

        @pl.when(k > 0)
        def _():
            dual_update(nxt, s, half)

        if half == 0:
            @pl.when(k > 0)
            def _():
                for side in range(2):
                    halo_copy(now, side, s).wait_recv()
                prim_v[now, s, PAD - 1:PAD, :] = hr_v[now, 0, s] * keep_left
                prim_v[now, s, PAD + HOURS_LOCAL:PAD + HOURS_LOCAL + 1, :] = hr_v[now, 1, s] * keep_right

            @pl.when(k == 0)
            def _():
                if s == 0:
                    for cp in start_halo:
                        cp.wait()
                for src in range(2):
                    lanes = slice(COLS_CORE * src, COLS_CORE * (src + 1))
                    prim_v[0, s, PAD - 1:PAD, lanes] = h0r_v[0, src, s] * keep_left
                    prim_v[0, s, PAD + HOURS_LOCAL:PAD + HOURS_LOCAL + 1, lanes] = h0r_v[1, src, s] * keep_right
        else:
            @pl.when(k == 0)
            def _():
                for cp in swap_s[s]:
                    cp.wait()

        dual = rows_of(pre_v, s, half)
        low = dual.astype(BF16)
        image = None
        for j in range(4):
            cols = slice(256 * j, 256 * (j + 1))
            pulled_all = jnp.dot(low, m_v[:, cols], preferred_element_type=F32)
            sb = jnp.concatenate([sb_v[s, 2 * j:2 * j + 1, :], sb_v[s, 2 * j + 1:2 * j + 2, :]], axis=1)
            exts = []
            at = 0
            for r0, n in PARTS[half]:
                pulled = pulled_all[at:at + n]
                at += n
                p = prim_v[now, s, PAD + r0:PAD + r0 + n, cols]
                up = prim_v[now, s, PAD + r0 - 1:PAD + r0 + n - 1, cols]
                down = prim_v[now, s, PAD + r0 + 1:PAD + r0 + n + 1, cols]
                cap = jnp.maximum(a_v[s, r0:r0 + n, cols] - sb, 0.0)
                rest = (cost_v[s, r0:r0 + n, cols] - pulled) + cap
                fresh = (
                    (1.0 - 2.0 * RAMP_WEIGHT * STEP_PRIMAL) * p
                    + (RAMP_WEIGHT * STEP_PRIMAL) * (up + down)
                    - STEP_PRIMAL * rest
                )
                fresh = jnp.maximum(fresh, 0.0)
                ext = 2.0 * fresh - p
                prim_v[nxt, s, PAD + r0:PAD + r0 + n, cols] = fresh
                a_v[s, r0:r0 + n, cols] = cap + STEP_CAP * ext
                exts.append(ext)
            ext_all = exts[0] if len(exts) == 1 else jnp.concatenate(exts, axis=0)
            part = jnp.dot(ext_all.astype(BF16), mt_v[cols, :], preferred_element_type=F32)
            image = part if image is None else image + part

        if half == 0:
            @pl.when(k < ITERS - 1)
            def _():
                for side, row in ((0, PAD), (1, PAD + HOURS_LOCAL - 1)):
                    @pl.when(k > 0)
                    def _():
                        halo_copy(nxt, side, s).wait_send()

                    he_v[side, s] = prim_v[nxt, s, row:row + 1, :]
                    halo_copy(nxt, side, s).start()

        @pl.when(k > 0)
        def _():
            image_copy(now, s, half).wait_send()

        at, m = SENT[half]
        xs_v[s, at:at + m, :] = jnp.concatenate([image[:, :128], image[:, 128:]], axis=0).astype(BF16)
        image_copy(now, s, half).start()
        put_rows(pre_v, s, half, dual + STEP_DUAL * (rows_of(dem_v, s, half) - image))

    def invest_step(total, s):
        mean = total * (1.0 / (NH * HOURS_LOCAL))
        spent = None
        for g in range(3):
            inv = invs_v[s, g]
            grad = base_v[s, g] + PENALTY * inv - mean
            new = jnp.maximum(inv - STEP_INVEST * grad, 0.0)
            invs_v[s, g] = new
            ext = 2.0 * new - inv
            spent = ext if spent is None else spent + ext
        sb_v[s] = STEP_CAP * spent

    def sums_in(k, now):
        @pl.when(k == 0)
        def _():
            for cp in first:
                cp.wait()
            for s in range(2):
                parts = []
                for src in range(2):
                    total = p0r_v[src, 0, s]
                    for h in range(1, NH):
                        total = total + p0r_v[src, h, s]
                    parts.append(total)
                invest_step(jnp.concatenate(parts, axis=0), s)

        @pl.when(k > 0)
        def _():
            all_sums(now, precv).wait()
            parts = [pr_v[now, h].astype(F32) for h in range(NH)]
            while len(parts) > 1:
                parts = [parts[i] + parts[i + 1] for i in range(0, len(parts), 2)]
            for s in range(2):
                invest_step(parts[0][8 * s:8 * (s + 1)], s)

    def step(k, carry):
        now = lax.rem(k, 2)
        nxt = 1 - now
        for s in range(2):
            for half in (1, 0):
                chunk(k, now, s, half)
        sums_in(k, now)

        @pl.when(k < ITERS - 1)
        def _():
            for s in range(2):
                for j in range(8):
                    left_over = jnp.maximum(a_v[s, :, 128 * j:128 * (j + 1)] - sb_v[s, j:j + 1, :], 0.0)
                    at = 8 * s + j
                    sum_v[at:at + 1, :] = jnp.sum(left_over, axis=0, keepdims=True)
            pr_v[nxt, h_at] = sum_v[...].astype(BF16)
            for d in order:
                sum_copy(nxt, d).start()

        @pl.when(k > 0)
        def _():
            all_sums(now, psend).wait()

        @pl.when(k == 0)
        def _():
            coefficients()

        @pl.when(k == ITERS - 1)
        def _():
            g_v[0, core] = invs_v[...]

        return carry

    prepare()
    lax.fori_loop(0, ITERS, step, 0)

    gathers = [
        send(g_v.at[0, core], g_v.at[1, core], gsend.at[1], grecv.at[1], peer_o0),
        send(g_v.at[0, core], g_v.at[1, core], gsend.at[2], grecv.at[2], peer_o1),
        send(g_v.at[0, core], g_v.at[0, core], gsend.at[0], grecv.at[0], peer_core),
    ]
    end = ITERS % 2
    outs = [
        send(
            prim_v.at[end, :, body_rows, pl.ds(pl.multiple_of(other * COLS_CORE, COLS_CORE), COLS_CORE)],
            disp_o.at[own_pair], osend.at[0], orecv.at[0], peer_core,
        )
    ]
    c_own = pltpu.make_async_copy(prim_v.at[end, :, body_rows, own_cols], disp_o.at[own_pair], oload.at[0])
    c_own.start()

    on_first = jnp.where(r_at < 2, 1.0, 0.0).astype(F32) > 0.5
    for s in range(2):
        for half in range(2):
            image_copy(1 - end, s, half).wait_send()
            dual_update(1 - end, s, half)
        d = pre_v[s]
        d = jnp.where(on_first, d[:, :128], d[:, 128:]).T
        lo, hi = d[:64], d[64:]
        do_v[0, s] = jnp.where(core == 0, lo, hi)
        do_v[1, s] = jnp.where(core == 0, hi, lo)
    outs.append(send(do_v.at[1], dual_o.at[own_pair], osend.at[1], orecv.at[1], peer_core))
    c_dual_own = pltpu.make_async_copy(do_v.at[0], dual_o.at[own_pair], oload.at[1])
    c_dual_own.start()
    for side in range(2):
        for s in range(2):
            halo_copy(end, side, s).wait_send()

    for cp in gathers[::-1]:
        cp.wait()
    for g in range(3):
        invs = [g_v[t // 4, (t // 2) % 2, t % 2, g] for t in range(8)]
        for s in range(4):
            spread = None
            for t in range(8):
                at = (3 * s + g) * 8 + t
                term = co_v[at:at + 1, :] * invs[t]
                spread = term if spread is None else spread + term
            tmp_v[0, 3 * s + g] = invs[s]
            tmp_v[1, 3 * s + g] = PENALTY * (invs[s] - spread)
    for s in range(4):
        for g in range(3):
            for i in range(4):
                lanes = slice(128 * i, 128 * (i + 1))
                inv_o[g, s:s + 1, lanes] = tmp_v[0, 3 * s + g, pl.ds(4 * core + i, 1), :]
                mult_o[g, s:s + 1, lanes] = il_v[1, g, s:s + 1, lanes] + tmp_v[1, 3 * s + g, pl.ds(4 * core + i, 1), :]
    for cp in outs:
        cp.wait()
    c_own.wait()
    c_dual_own.wait()


def hand_over(disp_i, dual_i, inv_i, mult_i, disp_o, dual_o, inv_o, mult_o, sem):
    copies = []
    pairs = [(inv_i, inv_o), (mult_i, mult_o)]
    for s in range(4):
        pairs.append((disp_i.at[s], disp_o.at[s]))
    pairs.append((dual_i, dual_o))
    for n, (src, dst) in enumerate(pairs):
        copies.append(pltpu.make_async_copy(src, dst, sem.at[n]))
    for cp in copies:
        cp.start()
    for cp in copies:
        cp.wait()


def shards(*args):
    args = args[:8] + tuple(jnp.transpose(x, (1, 0, 2)) for x in args[8:11]) + args[11:]
    hbm = pl.BlockSpec(memory_space=pltpu.HBM)
    vmem = pl.BlockSpec(memory_space=pltpu.VMEM)
    dma = pltpu.SemaphoreType.DMA
    disp, dual, inv, mult = pl.pallas_call(
        kernel,
        out_shape=(
            pltpu.VMEM((4, HOURS_LOCAL, COLS_CORE), F32),
            pltpu.VMEM((4, 64, HOURS_LOCAL), F32),
            pltpu.VMEM((3, 4, COLS_CORE), F32),
            pltpu.VMEM((3, 4, COLS_CORE), F32),
        ),
        in_specs=[hbm] * 13,
        out_specs=(vmem,) * 4,
        scratch_shapes=[
            pltpu.VMEM((2, HOURS_LOCAL, COLS), F32),
            pltpu.VMEM((2, 2, HOURS_LOCAL + 2 * PAD, COLS), F32),
            pltpu.VMEM((2, HOURS_LOCAL, COLS), F32),
            pltpu.VMEM((4, HOURS_LOCAL, COLS_CORE), F32),
            pltpu.VMEM((CONS, COLS_CORE), BF16),
            pltpu.VMEM((CONS, COLS_CORE), jnp.int32),
            pltpu.VMEM((CONS, COLS_CORE), BF16),
            pltpu.VMEM((CONS, COLS), BF16),
            pltpu.VMEM((COLS, CONS), BF16),
            pltpu.VMEM((2, HOURS_LOCAL, CONS), F32),
            pltpu.VMEM((2, HOURS_LOCAL, CONS), F32),
            pltpu.VMEM((2, 2 * HOURS_LOCAL, 128), BF16),
            pltpu.VMEM((2, 2, 2 * HOURS_LOCAL, 128), BF16),
            pltpu.VMEM((2, NH, 16, 128), BF16),
            pltpu.VMEM((2, 2, 4, 128), F32),
            pltpu.VMEM((2, NH, 2, 4, 128), F32),
            pltpu.VMEM((2, 2, 1, COLS), F32),
            pltpu.VMEM((2, 2, 2, 1, COLS), F32),
            pltpu.VMEM((2, 4, 8, COLS_CORE), F32),
            pltpu.VMEM((2, 4, 1, COLS_CORE), F32),
            pltpu.VMEM((2, 2, 2, 1, COLS_CORE), F32),
            pltpu.VMEM((3, 3, 4, COLS_CORE), F32),
            pltpu.VMEM((3, COLS_CORE), F32),
            pltpu.VMEM((2, 2, 2, 3, 4, 128), F32),
            pltpu.VMEM((2, 2, 3, 4, 128), F32),
            pltpu.VMEM((2, 3, 8, 128), F32),
            pltpu.VMEM((2, 3, 8, 128), F32),
            pltpu.VMEM((2, 8, 128), F32),
            pltpu.VMEM((16, 128), F32),
            pltpu.VMEM((16, 128), F32),
            pltpu.VMEM((96, 128), F32),
            pltpu.VMEM((2, 2, 2, 3, 8, 128), F32),
            pltpu.VMEM((2, 12, 8, 128), F32),
            pltpu.VMEM((2, 2, 64, HOURS_LOCAL), F32),
            pltpu.VMEM((16, 128), F32),
            pltpu.SMEM((4,), F32),
            pltpu.SMEM((3, 4), jnp.int32),
            dma((17,)),
            dma((2, 2)), dma((2, 2, 2)),
            dma((2,)), dma((2,)),
            dma((2, NH)), dma((2, NH)),
            dma((2, 2)), dma((2, 2, 2)),
            dma((2, 2)), dma((2, 2)),
            dma((9,)), dma((9,)),
            dma((3,)), dma((3,)),
            dma((2,)), dma((2,)), dma((2,)),
        ],
        compiler_params=pltpu.CompilerParams(
            collective_id=0, has_side_effects=True, vmem_limit_bytes=58 * 2**20
        ),
        cost_estimate=pl.CostEstimate(flops=3 * 10**9, bytes_accessed=9 * 10**6, transcendentals=0),
    )(*args)
    disp, dual, inv, mult = pl.pallas_call(
        hand_over,
        out_shape=tuple(jax.ShapeDtypeStruct(x.shape, x.dtype) for x in (disp, dual, inv, mult)),
        in_specs=[vmem] * 4,
        out_specs=(hbm,) * 4,
        scratch_shapes=[dma((7,))],
        compiler_params=pltpu.CompilerParams(vmem_limit_bytes=2**20),
        cost_estimate=pl.CostEstimate(flops=0, bytes_accessed=3 * 10**6, transcendentals=0),
    )(disp, dual, inv, mult)
    return disp, jnp.transpose(dual, (0, 2, 1)), jnp.transpose(inv, (1, 0, 2)), jnp.transpose(mult, (1, 0, 2))


def solution(mesh):
    placed = (
        P("scen", "hour", "reg"),
        P(None, "reg"),
        P("hour", None, "reg"),
        P("hour", None, "reg"),
        P("scen", "hour", None),
        P("scen", "hour", "reg"),
        P("scen", "hour", None),
        P("scen", "hour", "reg"),
        P("scen", None, "reg"),
        P("scen", None, "reg"),
        P("scen", None, "reg"),
        P("scen"),
        P(None, "scen"),
    )
    return jax.shard_map(
        shards,
        mesh=mesh,
        in_specs=placed,
        out_specs=(
            P("scen", "hour", "reg"),
            P("scen", "hour", "reg"),
            P("scen", None, "reg"),
            P("scen", None, "reg"),
        ),
        check_vma=False,
    )
```
